128 devices in a mesh: dp: 16 (over x, z_hi, core), seq: 8 (over z_lo, y).
Axes of the slice: x: 4, y: 4, z: 4 (z_hi: 2, z_lo: 2; z = z_hi * 2 + z_lo), core: 2. Of those that a mesh axis runs over, the one named last changes fastest.
Arguments:
- queries: bfloat16 [16, 1024, 4096], P('dp', 'seq'), may hold values from -6 to 6
- key_input: bfloat16 [16, 1024, 4096], P('dp', 'seq'), may hold values from -6 to 6
- value_input: bfloat16 [16, 1024, 4096], P('dp', 'seq'), may hold values from -6 to 6
- cotangent: bfloat16 [16, 1024, 4096], P('dp', 'seq'), may hold values from -6 to 6
- out_weight: bfloat16 [4096, 4096], P('dp', 'seq'), may hold values from -0.09375 to 0.09375
- filters: bfloat16 [256, 128], replicated, may hold values from -0.5 to 0.5
- skip_gain: float32 [4096], replicated, may hold values from -1 to 1
Outputs:
- grad_queries: bfloat16 [16, 1024, 4096], P('dp', 'seq')
- grad_keys: bfloat16 [16, 1024, 4096], P('dp', 'seq')
- grad_values: bfloat16 [16, 1024, 4096], P('dp', 'seq')
- grad_weight: float32 [4096, 4096], P('dp', 'seq')
- grad_filters: float32 [256, 128], P('seq')
- grad_gain: float32 [4096], P('seq')
The draws below stay inside these ranges and needn't reach their ends.
All inputs are finite; a program needn't handle non-finite values.
Results may differ from the reference program's by a relative error of at most 0.0095.
Values may be sent and summed in bfloat16 or wider, within the bound.
No kernel may reach another device: no remote copies, remote signals or barrier semaphores. Data moves between devices by JAX's collectives and lax.ppermute only.
A program may use at most 192 MiB of HBM per device.

```python
import math
import jax
import jax.numpy as jnp
from jax import lax

CH = 4096
DO = 4096
GROUP = 16
TAPS = 128
G = 256
SEQS = 16
LEN = 1024


def spiked(values, key, source, target, shards_of, factor):
    owner, partner = [(jnp.arange(values.shape[position]) // (values.shape[position] // shards_of)).reshape([-1 if axis == position else 1 for axis in range(values.ndim)]) for position in (source, target)]
    chosen = jax.random.permutation(key, shards_of)[partner]
    strong = (owner == chosen) | (owner == (partner + shards_of // 2) % shards_of)
    return jnp.where(strong, factor * values, values)


def block_levels(rng, dims, shards, smallest, high):
    gain = 1.0
    for position, parts in shards:
        steps = jax.random.uniform(jax.random.fold_in(jax.random.fold_in(rng, 6), position), (parts,), jnp.float32, smallest / len(shards), high / len(shards))
        gain = gain * jnp.repeat(jnp.exp(steps), dims[position] // parts).reshape((-1,) + (1,) * (len(dims) - 1 - position))
    return gain


def centred(key, shape, spread, most, shards=(), kind=jnp.bfloat16):
    entries = spread * jax.random.normal(key, shape, jnp.float32)
    if shards:
        entries = entries * block_levels(key, shape, shards, -0.22, 0.18)
    return jnp.clip(entries, -most, most).astype(kind)


def bell_draw_with(stream_key, shape, deviation, limit, cuts, heavy, dtype=jnp.bfloat16):
    entries = deviation * jax.random.normal(stream_key, shape, jnp.float32)
    if cuts:
        entries = entries * block_levels(stream_key, shape, cuts, -0.22, 0.18)
    return jnp.clip(spiked(entries, jax.random.fold_in(stream_key, 3), *heavy), -limit, limit).astype(dtype)


def setup_inputs(seed: int = 0) -> dict:
    streams_of = jax.random.split(jax.random.key(seed), 8)
    queries = centred(streams_of[0], (SEQS, LEN, CH), 1.0, 6.0, ((0, 16), (1, 8)))
    key_input = centred(streams_of[1], (SEQS, LEN, CH), 1.0, 6.0, ((0, 16), (1, 8)))
    value_input = centred(streams_of[2], (SEQS, LEN, CH), 1.0, 6.0, ((0, 16), (1, 8)))
    cotangent = bell_draw_with(streams_of[3], (SEQS, LEN, DO), 1.0, 6.0, ((0, 16), (1, 8)), (0, 2, 16, 2.0))
    out_weight = centred(streams_of[4], (DO, CH), CH ** -0.5, 0.09375, ((0, 16), (1, 8)))
    filters = centred(streams_of[5], (G, TAPS), TAPS ** -0.5, 0.5)
    skip_gain = jnp.clip(jax.random.uniform(streams_of[6], (CH,), jnp.float32, -1.0, 1.0), -1.0, 1.0)
    return {"queries": queries, "key_input": key_input, "value_input": value_input, "cotangent": cotangent, "out_weight": out_weight, "filters": filters, "skip_gain": skip_gain}


def causal_mix(mixed, taps_table):
    padded = jnp.concatenate([jnp.zeros((TAPS, mixed.shape[1]), jnp.float32), mixed], 0)

    def add_lag(lag, total):
        moved = lax.dynamic_slice_in_dim(padded, TAPS - lag, mixed.shape[0], 0)
        return total + taps_table[lag] * moved
    return lax.fori_loop(0, TAPS, add_lag, jnp.zeros_like(mixed))

def anti_mix(mixed, taps_table):
    padded = jnp.concatenate([mixed, jnp.zeros((TAPS, mixed.shape[1]), jnp.float32)], 0)

    def add_lag(lag, total):
        moved = lax.dynamic_slice_in_dim(padded, lag, mixed.shape[0], 0)
        return total + taps_table[lag] * moved
    return lax.fori_loop(0, TAPS, add_lag, jnp.zeros_like(mixed))

def lag_products(gradient, mixed):
    padded = jnp.concatenate([jnp.zeros((TAPS, mixed.shape[1]), jnp.float32), mixed], 0)

    def one_lag(lag, total):
        moved = lax.dynamic_slice_in_dim(padded, TAPS - lag, mixed.shape[0], 0)
        column = lax.optimization_barrier(jnp.sum(gradient * moved, 0)).reshape(G, GROUP).sum(1)
        return total.at[lag].set(column)
    return lax.fori_loop(0, TAPS, one_lag, jnp.zeros((TAPS, G), jnp.float32)).T

def reference(queries, key_input, value_input, cotangent, out_weight, filters, skip_gain):
    taps_table = jnp.repeat(filters.astype(jnp.float32), GROUP, axis=0).T
    scale = 1.0 / math.sqrt(SEQS * LEN)

    def one_sequence(carry, inputs):
        query, keyed, valued, grad_out = inputs
        product = (keyed.astype(jnp.float32) * valued.astype(jnp.float32)).astype(jnp.bfloat16)
        product_f = product.astype(jnp.float32)
        mixed = causal_mix(product_f, taps_table) + skip_gain * product_f
        gated = (query.astype(jnp.float32) * mixed).astype(jnp.bfloat16)
        grad_gated = jnp.dot(grad_out, out_weight, preferred_element_type=jnp.float32)
        grad_query = (grad_gated * mixed).astype(jnp.bfloat16)
        grad_mixed = (grad_gated * query.astype(jnp.float32)).astype(jnp.bfloat16)
        grad_mixed_f = grad_mixed.astype(jnp.float32)
        grad_product = anti_mix(grad_mixed_f, taps_table) + skip_gain * grad_mixed_f
        grad_key = (grad_product * valued.astype(jnp.float32)).astype(jnp.bfloat16)
        grad_value = (grad_product * keyed.astype(jnp.float32)).astype(jnp.bfloat16)
        weight_acc, filter_acc, gain_acc = carry
        weight_acc = weight_acc + lax.dot_general(grad_out, gated, (((0,), (0,)), ((), ())), preferred_element_type=jnp.float32)
        filter_acc = filter_acc + lag_products(grad_mixed_f, product_f)
        gain_acc = gain_acc + lax.optimization_barrier(jnp.sum(grad_mixed_f * product_f, 0))
        return ((weight_acc, filter_acc, gain_acc), (grad_query, grad_key, grad_value))
    start = (jnp.zeros((DO, CH), jnp.float32), jnp.zeros((G, TAPS), jnp.float32), jnp.zeros((CH,), jnp.float32))
    sums, grads = lax.scan(one_sequence, start, (queries, key_input, value_input, cotangent))
    return (grads[0], grads[1], grads[2], sums[0] * scale, sums[1] * scale, sums[2] * scale)
```

```python
import functools
import math

import jax
import jax.numpy as jnp
from jax import lax
from jax.experimental import pallas as pl
from jax.experimental.pallas import tpu as pltpu
from jax.sharding import Mesh
from jax.sharding import PartitionSpec as P

GROUP = 16
TAPS = 128
BLOCKS = 8
BF = jnp.bfloat16
F32 = jnp.float32
MIB = 1024 * 1024
DP = ("x", "zh", "core")
SEQ = ("zl", "y")

ANY = pl.BlockSpec(memory_space=pl.ANY)
SMEM = pl.BlockSpec(memory_space=pltpu.SMEM)
VMEM = pl.BlockSpec(memory_space=pltpu.VMEM)


def call(body, out_shape, in_specs, out_specs, scratch=(), flops=0, moved=0, limit=40):
    return pl.pallas_call(
        body,
        out_shape=out_shape,
        in_specs=in_specs,
        out_specs=out_specs,
        scratch_shapes=list(scratch),
        compiler_params=pltpu.CompilerParams(vmem_limit_bytes=limit * MIB),
        cost_estimate=pl.CostEstimate(flops=flops, bytes_accessed=moved, transcendentals=0),
    )


def shape(dims, dtype=BF):
    return jax.ShapeDtypeStruct(dims, dtype)


def transpose_kernel(w_ref, out_ref):
    out_ref[...] = w_ref[...].astype(F32).T.astype(BF)


def table_kernel(panel_ref, filters_ref, gain_ref, table_ref, gain_out_ref):
    groups = table_ref.shape[0]
    panel = panel_ref[0]
    row = lax.broadcasted_iota(jnp.int32, (8, 2 * TAPS), 0)
    first = pl.multiple_of(panel * groups, groups)
    taps_all = filters_ref[pl.ds(first, groups), :].astype(F32)
    for g in range(groups):
        taps = jnp.broadcast_to(taps_all[g : g + 1, :], (8, TAPS))
        rows = jnp.concatenate([taps, jnp.zeros((8, TAPS), F32)], 1)
        for bit in (1, 2, 4):
            rows = jnp.where((row & bit) != 0, pltpu.roll(rows, bit, 1), rows)
        count = 8
        while count < TAPS:
            rows = jnp.concatenate([rows, pltpu.roll(rows, count, 1)], 0)
            count *= 2
        table_ref[g] = rows.astype(BF)
    gain_rows = gain_ref[panel]
    for i in range(gain_rows.shape[0]):
        gain_out_ref[TAPS * i : TAPS * (i + 1), :] = jnp.broadcast_to(
            gain_rows[i : i + 1, :], (TAPS, TAPS)
        ).T


def prepare_kernel(channels_ref, q_ref, k_ref, v_ref, *outs):
    width = outs[0].shape[1]
    for j in range(BLOCKS):
        cols = pl.ds(pl.multiple_of(channels_ref[j] * width, width), width)
        product = k_ref[:, cols].astype(F32) * v_ref[:, cols].astype(F32)
        outs[j][0] = product.T.astype(BF)
        outs[j][1] = q_ref[:, cols].astype(F32).T.astype(BF)


def tiles(rows):
    return [rows[:, TAPS * b : TAPS * (b + 1)] for b in range(BLOCKS)]


def forward_kernel(place_ref, *refs):
    slots = refs[:BLOCKS]
    table_ref, gain_ref, p_ref, q_ref, mixed_ref, gated_ref, sems = refs[BLOCKS:]
    copies = []
    for j in range(BLOCKS):
        lanes = pl.ds(pl.multiple_of(place_ref[j] * TAPS, TAPS), TAPS)
        for i, dst in ((0, p_ref), (1, q_ref)):
            copies.append(pltpu.make_async_copy(slots[j].at[i], dst.at[:, lanes], sems.at[2 * j + i]))
    for c in copies:
        c.start()
    for c in copies:
        c.wait()

    def one_group(g, carry):
        rows = pl.ds(pl.multiple_of(g * GROUP, GROUP), GROUP)
        x = tiles(p_ref[rows, :])
        q = tiles(q_ref[rows, :])
        zero = jnp.zeros((GROUP, TAPS), BF)
        lhs = jnp.concatenate(
            [jnp.concatenate(x, 0), jnp.concatenate([zero] + x[:-1], 0)], 1
        )
        table = table_ref[g]
        rhs = jnp.concatenate([table[:, :TAPS], table[:, TAPS:]], 0)
        conv = jnp.dot(lhs, rhs, preferred_element_type=F32)
        gain = gain_ref[rows, :]
        for b in range(BLOCKS):
            mixed = conv[GROUP * b : GROUP * (b + 1)] + gain * x[b].astype(F32)
            mixed_ref[rows, TAPS * b : TAPS * (b + 1)] = mixed
            gated_ref[rows, TAPS * b : TAPS * (b + 1)] = (q[b].astype(F32) * mixed).astype(BF)
        return carry

    lax.fori_loop(0, table_ref.shape[0], one_group, 0, unroll=4)


def cot_copies(place_ref, refs, held, sems):
    copies = []
    half = TAPS // 2
    for core in range(2):
        own, up, down, far_a, far_b = refs[5 * core : 5 * core + 5]
        for piece, (ref, k, first, count) in enumerate(
            ((own, 0, 0, TAPS), (up, 1, 0, TAPS), (down, 3, 0, TAPS), (far_a, 2, 0, half), (far_b, 2, half, half))
        ):
            start = pl.multiple_of(place_ref[4 * core + k] * TAPS + first, half)
            copies.append(
                pltpu.make_async_copy(ref, held.at[pl.ds(start, count), :], sems.at[5 * core + piece])
            )
    return copies


def weight_kernel(place_ref, at_ref, *refs):
    cot = refs[:10]
    gated_ref = refs[10]
    out_x = refs[11:15]
    out_z = refs[15:19]
    held, sems = refs[19:]
    copies = cot_copies(place_ref, cot, held, sems)
    for c in copies:
        c.start()
    for c in copies:
        c.wait()
    half = gated_ref.shape[0] // 2
    width = out_x[0].shape[2]
    x, z = at_ref[0], at_ref[1]
    for k in range(4):
        xk = lax.rem(x + k, 4)
        zk = lax.rem(z + k, 4)

        def part(i, carry, xk=xk, zk=zk, k=k):
            cols = pl.ds(pl.multiple_of((xk * 4 + i) * width, width), width)
            out_x[k][i] = jnp.dot(
                gated_ref[:half, :], held[:, cols], preferred_element_type=F32
            ).astype(BF)
            cols = pl.ds(pl.multiple_of((i * 4 + zk) * width, width), width)
            out_z[k][i] = jnp.dot(
                gated_ref[half:, :], held[:, cols], preferred_element_type=F32
            ).astype(BF)
            return carry

        lax.fori_loop(0, 4, part, 0)


def gradient_kernel(place_ref, *refs):
    cot = refs[:10]
    w_ref, mixed_ref, q_ref = refs[10:13]
    gm_ref = refs[13]
    outs = refs[14:22]
    held, w_held, gq, sems, w_sems, out_sems = refs[22:]
    copies = cot_copies(place_ref, cot, held, sems)
    blocks, channels, width = w_ref.shape
    for d in range(blocks):
        copies.append(
            pltpu.make_async_copy(w_ref.at[d], w_held.at[:, width * d : width * (d + 1)], w_sems.at[d])
        )
    for c in copies:
        c.start()
    for c in copies:
        c.wait()
    span = 2 * TAPS

    def part(n, carry):
        toks = pl.ds(pl.multiple_of(n * span, span), span)
        grad = lax.dot_general(
            w_held[...], held[toks, :], (((1,), (1,)), ((), ())), preferred_element_type=F32
        )
        gq[:, toks] = (grad * mixed_ref[:, toks]).astype(BF)
        gm_ref[:, toks] = (grad * q_ref[:, toks].astype(F32)).astype(BF)
        return carry

    lax.fori_loop(0, held.shape[0] // span, part, 0)
    backs = []
    for j in range(BLOCKS):
        lanes = pl.ds(pl.multiple_of(place_ref[j] * TAPS, TAPS), TAPS)
        backs.append(pltpu.make_async_copy(gq.at[:, lanes], outs[j], out_sems.at[j]))
    for c in backs:
        c.start()
    for c in backs:
        c.wait()


def backward_kernel(place_ref, gm_ref, table_ref, gain_ref, *refs):
    outs = refs[:BLOCKS]
    gp, out_sems = refs[BLOCKS:]

    def one_group(g, carry):
        rows = pl.ds(pl.multiple_of(g * GROUP, GROUP), GROUP)
        x = tiles(gm_ref[rows, :])
        zero = jnp.zeros((GROUP, TAPS), BF)
        lhs = jnp.concatenate(
            [jnp.concatenate(x, 0), jnp.concatenate(x[1:] + [zero], 0)], 1
        )
        conv = lax.dot_general(
            lhs, table_ref[g], (((1,), (1,)), ((), ())), preferred_element_type=F32
        )
        gain = gain_ref[rows, :]
        for b in range(BLOCKS):
            total = conv[GROUP * b : GROUP * (b + 1)] + gain * x[b].astype(F32)
            gp[rows, TAPS * b : TAPS * (b + 1)] = total.astype(BF)
        return carry

    lax.fori_loop(0, table_ref.shape[0], one_group, 0, unroll=4)
    backs = []
    for j in range(BLOCKS):
        lanes = pl.ds(pl.multiple_of(place_ref[j] * TAPS, TAPS), TAPS)
        backs.append(pltpu.make_async_copy(gp.at[:, lanes], outs[j], out_sems.at[j]))
    for c in backs:
        c.start()
    for c in backs:
        c.wait()


def filter_kernel(gm_ref, p_ref, out_ref):
    groups = gm_ref.shape[0] // GROUP
    span = 2 * TAPS
    row = lax.broadcasted_iota(jnp.int32, (8, span), 0)

    def one_group(g, carry):
        rows = pl.ds(pl.multiple_of(g * GROUP, GROUP), GROUP)
        x = jnp.concatenate(tiles(p_ref[rows, :]), 0)
        y = tiles(gm_ref[rows, :])
        zero = jnp.zeros((GROUP, TAPS), BF)
        window = jnp.concatenate(
            [jnp.concatenate(y, 0), jnp.concatenate(y[1:] + [zero], 0)], 1
        )
        pairs = lax.dot_general(x, window, (((0,), (0,)), ((), ())), preferred_element_type=F32)
        count = TAPS
        while count > 8:
            count //= 2
            pairs = pairs[:count] + pltpu.roll(pairs[count:], span - count, 1)
        for bit in (4, 2, 1):
            pairs = jnp.where((row & bit) != 0, pltpu.roll(pairs, span - bit, 1), pairs)
        out_ref[pl.ds(g, 1), :] = jnp.sum(pairs, 0, keepdims=True)[:, :TAPS]
        return carry

    lax.fori_loop(0, groups, one_group, 0, unroll=2)
    channels = gm_ref.shape[0]
    for i in range(channels // TAPS):
        rows = slice(TAPS * i, TAPS * (i + 1))
        total = jnp.zeros((TAPS, TAPS), F32)
        for b in range(BLOCKS):
            lanes = slice(TAPS * b, TAPS * (b + 1))
            total += gm_ref[rows, lanes].astype(F32) * p_ref[rows, lanes].astype(F32)
        out_ref[groups + i : groups + i + 1, :] = jnp.sum(total.T, 0, keepdims=True)
    first = groups + channels // TAPS
    out_ref[first:, :] = jnp.zeros((out_ref.shape[0] - first, TAPS), F32)


def partial_kernel(at_ref, *refs):
    pieces, outs = refs[:4], refs[4:]
    for k in range(4):
        i = lax.rem(at_ref[0] + k, 4)
        total = pieces[0][i].astype(F32)
        for piece in pieces[1:]:
            total += piece[i].astype(F32)
        outs[k][...] = total.astype(BF)


def total_kernel(scale, *refs):
    out_ref = refs[8]
    for h in range(2):
        total = refs[4 * h][...].astype(F32)
        for ref in refs[4 * h + 1 : 4 * h + 4]:
            total += ref[...].astype(F32)
        half = total.shape[0]
        out_ref[:, half * h : half * (h + 1)] = (total * scale).T


def finish_kernel(channels_ref, k_ref, v_ref, *refs):
    gqs, gps = refs[:BLOCKS], refs[BLOCKS : 2 * BLOCKS]
    gq_ref, gk_ref, gv_ref = refs[2 * BLOCKS :]
    width = gqs[0].shape[0]
    for j in range(BLOCKS):
        cols = pl.ds(pl.multiple_of(channels_ref[j] * width, width), width)
        gq_ref[:, cols] = gqs[j][...].astype(F32).T.astype(BF)
        gp = gps[j][...].astype(F32).T
        gk_ref[:, cols] = (gp * v_ref[:, cols].astype(F32)).astype(BF)
        gv_ref[:, cols] = (gp * k_ref[:, cols].astype(F32)).astype(BF)


SWAP = [(0, 0), (1, 2), (2, 1), (3, 3)]
SLOTS = [(d, k) for d in range(2) for k in range(4)]


def ring(n, k):
    return [(i, (i + k) % n) for i in range(n)]


def stream_pairs(d, k):
    pairs = []
    for core in range(2):
        for zl in range(2):
            for y in range(4):
                pairs.append(((core * 2 + zl) * 4 + y, ((zl ^ d) * 2 + core) * 4 + (y + k) % 4))
    return pairs


def z_pairs(k):
    pairs = []
    for zh in range(2):
        for core in range(2):
            for zl in range(2):
                z = (zh * 2 + zl + k) % 4
                pairs.append(((zh * 2 + core) * 2 + zl, z * 2 + core))
    return pairs


def x_pairs(k):
    pairs = []
    for x in range(4):
        for core in range(2):
            for zl in range(2):
                pairs.append(((x * 2 + core) * 2 + zl, (((x + k) % 4) * 2 + zl) * 2 + core))
    return pairs


def ring_z(k):
    return [(z, (z + k) % 4) for z in range(4)]


def shards(queries, key_input, value_input, cotangent, out_weight, filters, skip_gain):
    q, k, v, cot = queries[0], key_input[0], value_input[0], cotangent[0]
    rows, width = q.shape
    panel = width // 8
    outs_here = out_weight.shape[0]
    length = rows * 8
    groups = panel // GROUP
    scale = 1.0 / math.sqrt(16 * length)
    x, zh, core, zl, y = (lax.axis_index(n) for n in ("x", "zh", "core", "zl", "y"))
    z = zh * 2 + zl
    channels = jnp.stack([(zl ^ d) * 4 + (y + i) % 4 for d, i in SLOTS]).astype(jnp.int32)
    place = jnp.stack([(core ^ d) * 4 + (y - i) % 4 for d, i in SLOTS]).astype(jnp.int32)
    own_panel = (core * 4 + y).astype(jnp.int32).reshape(1)
    at = jnp.stack([x, z]).astype(jnp.int32)
    at_x, at_z = x.astype(jnp.int32).reshape(1), z.astype(jnp.int32).reshape(1)

    w_t = call(transpose_kernel, shape((panel, outs_here)), [VMEM], VMEM, moved=2 * outs_here * panel * 2)(out_weight)
    w_t = lax.ppermute(w_t, ("core", "zl"), SWAP)
    w_all = lax.all_gather(w_t, ("x", "zh", "zl"), axis=0)

    own = lax.ppermute(cot, ("core", "zl"), SWAP)
    up = lax.ppermute(own, "y", ring(4, 1))
    down = lax.ppermute(own, "y", ring(4, -1))
    far_a = lax.ppermute(up[: rows // 2], "y", ring(4, 1))
    far_b = lax.ppermute(down[rows // 2 :], "y", ring(4, -1))
    cots = [own, up, down, far_a, far_b]
    cots = cots + [lax.ppermute(c, "core", ring(2, 1)) for c in cots]

    chunks = call(
        prepare_kernel,
        [shape((2, panel, rows))] * BLOCKS,
        [SMEM, VMEM, VMEM, VMEM],
        [VMEM] * BLOCKS,
        flops=8 * rows * width,
        moved=10 * rows * width,
    )(channels, q, k, v)
    slots = [
        lax.ppermute(c, ("core", "zl", "y"), stream_pairs(d, i)) for c, (d, i) in zip(chunks, SLOTS)
    ]
    table, gain = call(
        table_kernel,
        [shape((groups, TAPS, 2 * TAPS)), shape((panel, TAPS), F32)],
        [SMEM, VMEM, VMEM],
        [VMEM, VMEM],
        flops=groups * TAPS * 2 * TAPS * 4,
        moved=3 * MIB,
    )(own_panel, filters, skip_gain.reshape(8, panel // TAPS, TAPS))
    p_t, q_t, mixed, gated = call(
        forward_kernel,
        [shape((panel, length)), shape((panel, length)), shape((panel, length), F32), shape((panel, length))],
        [SMEM] + [ANY] * BLOCKS + [VMEM, VMEM],
        [VMEM] * 4,
        scratch=[pltpu.SemaphoreType.DMA((2 * BLOCKS,))],
        flops=2 * groups * TAPS * TAPS * 2 * TAPS,
        moved=12 * MIB,
    )(place, *slots, table, gain)

    cot_held = pltpu.VMEM((length, width), BF)
    ten = pltpu.SemaphoreType.DMA((10,))
    parts = call(
        weight_kernel,
        [shape((4, panel // 2, outs_here))] * 8,
        [SMEM, SMEM] + [ANY] * 10 + [VMEM],
        [VMEM] * 8,
        scratch=[cot_held, ten],
        flops=2 * length * width * panel,
        moved=13 * MIB,
    )(place, at, *cots, gated)
    by_x, by_z = parts[:4], parts[4:]
    by_x = [by_x[0]] + [lax.ppermute(by_x[i], "x", ring(4, i)) for i in (1, 2, 3)]
    by_z = [by_z[0]] + [lax.ppermute(by_z[i], ("zh", "zl"), ring_z(i)) for i in (1, 2, 3)]
    partial = call(
        partial_kernel,
        [shape((panel // 2, outs_here))] * 4,
        [SMEM] + [VMEM] * 4,
        [VMEM] * 4,
        flops=4 * panel * outs_here * 4,
        moved=3 * MIB,
    )
    by_x = partial(at_z, *by_x)
    by_z = partial(at_x, *by_z)
    by_x = [lax.ppermute(c, ("zh", "core", "zl"), z_pairs(i)) for i, c in enumerate(by_x)]
    by_z = [lax.ppermute(c, ("x", "core", "zl"), x_pairs(i)) for i, c in enumerate(by_z)]
    grad_weight = call(
        functools.partial(total_kernel, scale),
        shape((outs_here, panel), F32),
        [VMEM] * 8,
        VMEM,
        flops=10 * panel * outs_here,
        moved=2 * MIB,
    )(*by_x, *by_z)

    grads = call(
        gradient_kernel,
        [shape((panel, length))] + [shape((panel, rows))] * BLOCKS,
        [SMEM] + [ANY] * 11 + [VMEM] * 2,
        [VMEM] + [ANY] * BLOCKS,
        scratch=[
            cot_held,
            pltpu.VMEM((panel, width), BF),
            pltpu.VMEM((panel, length), BF),
            ten,
            pltpu.SemaphoreType.DMA((16,)),
            pltpu.SemaphoreType.DMA((BLOCKS,)),
        ],
        flops=2 * length * width * panel,
        moved=17 * MIB,
    )(place, *cots, w_all, mixed, q_t)
    gm, gqs = grads[0], grads[1:]
    gps = call(
        backward_kernel,
        [shape((panel, rows))] * BLOCKS,
        [SMEM] + [VMEM] * 3,
        [ANY] * BLOCKS,
        scratch=[pltpu.VMEM((panel, length), BF), pltpu.SemaphoreType.DMA((BLOCKS,))],
        flops=2 * groups * TAPS * TAPS * 2 * TAPS,
        moved=5 * MIB,
    )(place, gm, table, gain)

    def home(chunks):
        moved = []
        for c, (d, i) in zip(chunks, SLOTS):
            pairs = [(b, a) for a, b in stream_pairs(d, i)]
            moved.append(lax.ppermute(c, ("core", "zl", "y"), pairs))
        return moved

    gqs, gps = home(gqs), home(gps)
    sums = call(
        filter_kernel,
        shape((40, TAPS), F32),
        [VMEM, VMEM],
        VMEM,
        flops=2 * groups * TAPS * TAPS * 2 * TAPS,
        moved=3 * MIB,
    )(gm, p_t)
    sums = lax.all_gather(sums, ("x", "zh", "zl"), axis=0)
    sums = jnp.sum(sums, 0) * scale
    sums = lax.ppermute(sums, ("core", "zl"), SWAP)
    grad_filters = sums[:groups]
    grad_gain = sums[groups : groups + panel // TAPS].reshape(panel)

    grad_query, grad_key, grad_value = call(
        finish_kernel,
        [shape((rows, width))] * 3,
        [SMEM] + [VMEM] * 18,
        [VMEM] * 3,
        flops=10 * rows * width,
        moved=14 * rows * width,
    )(channels, k, v, *gqs, *gps)
    return (
        grad_query[None],
        grad_key[None],
        grad_value[None],
        grad_weight,
        grad_filters,
        grad_gain,
    )


def solution(mesh):
    fine = Mesh(mesh.devices.reshape(4, 2, 2, 2, 4), ("x", "zh", "core", "zl", "y"))
    stream = P(DP, SEQ, None)
    return jax.shard_map(
        shards,
        mesh=fine,
        in_specs=(stream, stream, stream, stream, P(DP, SEQ), P(), P()),
        out_specs=(stream, stream, stream, P(DP, SEQ), P(SEQ, None), P(SEQ)),
        check_vma=False,
    )
```

```python
import functools
import math

import jax
import jax.numpy as jnp
from jax import lax
from jax.experimental import pallas as pl
from jax.experimental.pallas import tpu as pltpu
from jax.sharding import Mesh
from jax.sharding import PartitionSpec as P

GROUP = 16
TAPS = 128
BLOCKS = 8
BF = jnp.bfloat16
F32 = jnp.float32
LIMIT = 60 * 1024 * 1024
DP = ("x", "zh", "core")
SEQ = ("zl", "y")

ANY = pl.BlockSpec(memory_space=pl.ANY)
SMEM = pl.BlockSpec(memory_space=pltpu.SMEM)
VMEM = pl.BlockSpec(memory_space=pltpu.VMEM)


def call(body, out_shape, in_specs, out_specs, scratch=(), micros=1):
    return pl.pallas_call(
        body,
        out_shape=out_shape,
        in_specs=in_specs,
        out_specs=out_specs,
        scratch_shapes=list(scratch),
        compiler_params=pltpu.CompilerParams(vmem_limit_bytes=LIMIT),
        cost_estimate=pl.CostEstimate(flops=1, bytes_accessed=micros * 3000000, transcendentals=0),
    )


def shape(dims, dtype=BF):
    return jax.ShapeDtypeStruct(dims, dtype)


def table_kernel(panel_ref, filters_ref, gain_ref, table_ref, gain_out_ref):
    groups = table_ref.shape[0]
    panel = panel_ref[0]
    row = lax.broadcasted_iota(jnp.int32, (8, 2 * TAPS), 0)
    first = pl.multiple_of(panel * groups, groups)
    taps_all = filters_ref[pl.ds(first, groups), :].astype(F32)
    for g in range(groups):
        taps = jnp.broadcast_to(taps_all[g : g + 1, :], (8, TAPS))
        rows = jnp.concatenate([taps, jnp.zeros((8, TAPS), F32)], 1)
        for bit in (1, 2, 4):
            rows = jnp.where((row & bit) != 0, pltpu.roll(rows, bit, 1), rows)
        count = 8
        while count < TAPS:
            rows = jnp.concatenate([rows, pltpu.roll(rows, count, 1)], 0)
            count *= 2
        table_ref[g] = rows.astype(BF)
    gain_rows = gain_ref[panel]
    for i in range(gain_rows.shape[0]):
        gain_out_ref[TAPS * i : TAPS * (i + 1), :] = jnp.broadcast_to(
            gain_rows[i : i + 1, :], (TAPS, TAPS)
        ).T


def transpose_kernel(w_ref, out_ref):
    out_ref[...] = w_ref[...].astype(F32).T.astype(BF)


def prepare_kernel(q_ref, k_ref, v_ref, out_ref):
    width = out_ref.shape[2]
    for j in range(out_ref.shape[0]):
        cols = slice(j * width, (j + 1) * width)
        product = k_ref[:, cols].astype(F32) * v_ref[:, cols].astype(F32)
        out_ref[j, 0] = product.T.astype(BF)
        out_ref[j, 1] = q_ref[:, cols].astype(F32).T.astype(BF)


def forward_kernel(slot_ref, pq_ref, table_ref, gain_ref, mixed_ref, gated_ref):
    def one_group(g, carry):
        rows = pl.ds(pl.multiple_of(g * GROUP, GROUP), GROUP)
        x = [pq_ref[b, 0, rows, :] for b in range(BLOCKS)]
        zero = jnp.zeros((GROUP, TAPS), BF)
        lhs = jnp.concatenate(
            [jnp.concatenate(x, 0), jnp.concatenate([zero] + x[:-1], 0)], 1
        )
        table = table_ref[g]
        rhs = jnp.concatenate([table[:, :TAPS], table[:, TAPS:]], 0)
        conv = jnp.dot(lhs, rhs, preferred_element_type=F32)
        gain = gain_ref[rows, :]
        for b in range(BLOCKS):
            mixed = conv[GROUP * b : GROUP * (b + 1)] + gain * x[b].astype(F32)
            mixed_ref[b, rows, :] = mixed
            lanes = pl.ds(pl.multiple_of(slot_ref[b] * TAPS, TAPS), TAPS)
            gated_ref[rows, lanes] = (pq_ref[b, 1, rows, :].astype(F32) * mixed).astype(BF)
        return carry

    lax.fori_loop(0, table_ref.shape[0], one_group, 0, unroll=4)


def cot_copies(refs, held, sem_of, cols=slice(None)):
    copies = []
    half = TAPS // 2
    for zl in range(2):
        own, up, down, far_a, far_b = refs[5 * zl : 5 * zl + 5]
        for ref, k, first, count in (
            (own, 0, 0, TAPS),
            (up, 1, 0, TAPS),
            (far_a, 2, 0, half),
            (far_b, 2, half, half),
            (down, 3, 0, TAPS),
        ):
            slot = 4 * zl + k
            rows = slice(slot * TAPS + first, slot * TAPS + first + count)
            copies.append(
                pltpu.make_async_copy(ref.at[:, cols], held.at[rows, cols], sem_of(slot))
            )
    return copies


def weight_kernel(core_ref, *refs):
    cot = refs[:10]
    gated_ref, mine_ref, other_ref, held, total, sems, out_sems = refs[10:]
    blocks, channels, width = mine_ref.shape
    stripes = sems.shape[0]
    span = held.shape[1] // stripes
    each = blocks // stripes
    for n in range(stripes):
        for c in cot_copies(cot, held, lambda slot, n=n: sems.at[n], slice(span * n, span * (n + 1))):
            c.start()

    def out_copies(n):
        part = pl.ds(n * each, each)
        return [
            pltpu.make_async_copy(total.at[lax.rem(core_ref[0] + i, 2), part], ref.at[part], out_sems.at[i, n])
            for i, ref in enumerate((mine_ref, other_ref))
        ]

    def stripe(n, carry):
        cols = pl.ds(pl.multiple_of(n * span, span), span)
        pltpu.make_async_copy(held.at[:, cols], held.at[:, cols], sems.at[n]).wait()
        for i in range(2 * each):
            cols = pl.ds(pl.multiple_of(n * span + i * width, width), width)
            total[i % 2, n * each + i // 2] = jnp.dot(
                gated_ref[...], held[:, cols], preferred_element_type=F32
            ).astype(BF)
        for c in out_copies(n):
            c.start()
        return carry

    lax.fori_loop(0, stripes, stripe, 0)
    for n in range(stripes):
        for c in out_copies(n):
            c.wait()


def gradient_kernel(place_ref, *refs):
    cot = refs[:10]
    w_ref, mixed_ref, pq_ref, table_ref, gain_ref, gm_ref, out_ref = refs[10:17]
    held, w_held, result, sems, w_sems, out_sems = refs[17:]
    blocks, channels, width = w_ref.shape
    weights = []
    for d in range(blocks):
        weights.append(
            pltpu.make_async_copy(w_ref.at[d], w_held.at[:, width * d : width * (d + 1)], w_sems.at[d])
        )
    for c in weights + cot_copies(cot, held, lambda slot: sems.at[slot // 2]):
        c.start()
    for c in weights:
        c.wait()
    span = 2 * TAPS

    def part(n, carry):
        toks = pl.ds(pl.multiple_of(n * span, span), span)
        pltpu.make_async_copy(held.at[toks, :], held.at[toks, :], sems.at[n]).wait()
        grad = lax.dot_general(
            w_held[...], held[toks, :], (((1,), (1,)), ((), ())), preferred_element_type=F32
        )
        for i in range(2):
            one = grad[:, TAPS * i : TAPS * (i + 1)]
            place = place_ref[2 * n + i]
            result[place, 0] = (one * mixed_ref[place]).astype(BF)
            gm_ref[place] = (one * pq_ref[place, 1].astype(F32)).astype(BF)
        return carry

    lax.fori_loop(0, held.shape[0] // span, part, 0)
    back = pltpu.make_async_copy(result.at[:, 0], out_ref.at[:, 0], out_sems.at[0])
    back.start()

    def one_group(g, carry):
        rows = pl.ds(pl.multiple_of(g * GROUP, GROUP), GROUP)
        x = [gm_ref[b, rows, :] for b in range(BLOCKS)]
        zero = jnp.zeros((GROUP, TAPS), BF)
        lhs = jnp.concatenate(
            [jnp.concatenate(x, 0), jnp.concatenate(x[1:] + [zero], 0)], 1
        )
        conv = lax.dot_general(
            lhs, table_ref[g], (((1,), (1,)), ((), ())), preferred_element_type=F32
        )
        gain = gain_ref[rows, :]
        for b in range(BLOCKS):
            total = conv[GROUP * b : GROUP * (b + 1)] + gain * x[b].astype(F32)
            result[b, 1, rows, :] = total.astype(BF)
        return carry

    lax.fori_loop(0, table_ref.shape[0], one_group, 0, unroll=4)
    rest = pltpu.make_async_copy(result.at[:, 1], out_ref.at[:, 1], out_sems.at[1])
    rest.start()
    back.wait()
    rest.wait()


def filter_kernel(gm_ref, pq_ref, out_ref):
    channels = gm_ref.shape[1]
    groups = channels // GROUP
    span = 2 * TAPS
    row = lax.broadcasted_iota(jnp.int32, (8, span), 0)

    def one_group(g, carry):
        rows = pl.ds(pl.multiple_of(g * GROUP, GROUP), GROUP)
        x = jnp.concatenate([pq_ref[b, 0, rows, :] for b in range(BLOCKS)], 0)
        y = [gm_ref[b, rows, :] for b in range(BLOCKS)]
        zero = jnp.zeros((GROUP, TAPS), BF)
        window = jnp.concatenate(
            [jnp.concatenate(y, 0), jnp.concatenate(y[1:] + [zero], 0)], 1
        )
        pairs = lax.dot_general(x, window, (((0,), (0,)), ((), ())), preferred_element_type=F32)
        count = TAPS
        while count > 8:
            count //= 2
            pairs = pairs[:count] + pltpu.roll(pairs[count:], span - count, 1)
        for bit in (4, 2, 1):
            pairs = jnp.where((row & bit) != 0, pltpu.roll(pairs, span - bit, 1), pairs)
        out_ref[pl.ds(g, 1), :] = jnp.sum(pairs, 0, keepdims=True)[:, :TAPS]
        return carry

    lax.fori_loop(0, groups, one_group, 0, unroll=8)
    for i in range(channels // TAPS):
        rows = slice(TAPS * i, TAPS * (i + 1))
        total = jnp.zeros((TAPS, TAPS), F32)
        for b in range(BLOCKS):
            total += gm_ref[b, rows, :].astype(F32) * pq_ref[b, 0, rows, :].astype(F32)
        out_ref[groups + i : groups + i + 1, :] = jnp.sum(total.T, 0, keepdims=True)
    first = groups + channels // TAPS
    out_ref[first:, :] = jnp.zeros((out_ref.shape[0] - first, TAPS), F32)


def pair_kernel(order_ref, mine_ref, other_ref, sums_ref, other_sums_ref, *outs):
    channels = mine_ref.shape[1]
    small = sums_ref[...] + other_sums_ref[...]
    high = small.astype(BF)
    low = (small - high.astype(F32)).astype(BF)
    for i, out in enumerate(outs):
        to = order_ref[i]
        out[:channels] = (mine_ref[to].astype(F32) + other_ref[to].astype(F32)).astype(BF)
        out[channels:, :TAPS] = high
        out[channels:, TAPS:] = low


def total_kernel(scale, source_ref, *refs):
    pieces = refs[:8]
    weight_ref, filter_ref, gain_ref, held = refs[8:]
    channels = weight_ref.shape[1]
    total = pieces[0][:channels].astype(F32)
    for piece in pieces[1:]:
        total += piece[:channels].astype(F32)
    weight_ref[...] = (total * scale).T
    for i, piece in enumerate(pieces):
        small = piece[channels:].astype(F32)
        held[source_ref[i]] = small[:, :TAPS] + small[:, TAPS:]
    total = held[0]
    for i in range(1, 8):
        total += held[i]
    total = total * scale
    groups = filter_ref.shape[0]
    filter_ref[...] = total[:groups]
    gain_ref[...] = total[groups : groups + gain_ref.shape[0]]


def finish_kernel(k_ref, v_ref, grads_ref, gq_ref, gk_ref, gv_ref):
    width = grads_ref.shape[2]
    for j in range(grads_ref.shape[0]):
        cols = slice(j * width, (j + 1) * width)
        gq_ref[:, cols] = grads_ref[j, 0].astype(F32).T.astype(BF)
        gp = grads_ref[j, 1].astype(F32).T
        gk_ref[:, cols] = (gp * v_ref[:, cols].astype(F32)).astype(BF)
        gv_ref[:, cols] = (gp * k_ref[:, cols].astype(F32)).astype(BF)


SLOTS = [(d, k) for d in range(2) for k in range(4)]
ROUTES = [(0, 0), (2, 1), (2, 0), (1, 1), (3, 1), (0, 1), (1, 0), (3, 0)]


def after(value, *others):
    return lax.optimization_barrier((value, *others))[0]


def ring(n, k):
    return [(i, (i + k) % n) for i in range(n)]


def route(k, d):
    return [(x * 2 + zh, (x + k) % 4 * 2 + (zh ^ d)) for x in range(4) for zh in range(2)]


def numbers(values):
    return jnp.stack(values).astype(jnp.int32)


def shards(queries, key_input, value_input, cotangent, out_weight, filters, skip_gain):
    q, k, v, cot = queries[0], key_input[0], value_input[0], cotangent[0]
    rows, width = q.shape
    half = rows // 2
    panel = width // 8
    outs_here = out_weight.shape[0]
    length = rows * 8
    groups = panel // GROUP
    scale = 1.0 / math.sqrt(16 * length)
    x, zh, core, zl, y = (lax.axis_index(n) for n in ("x", "zh", "core", "zl", "y"))
    place = numbers([(zl ^ d) * 4 + (y - i) % 4 for d, i in SLOTS])
    slot_of = numbers([(zl ^ (p // 4)) * 4 + (y - p) % 4 for p in range(BLOCKS)])
    order = numbers([(x + i) % 4 * 2 + (zh ^ d) for i, d in ROUTES])
    source = numbers([(x - i) % 4 * 2 + (zh ^ d) for i, d in ROUTES])
    stream = shape((8, 2, panel, rows))

    w_t = call(transpose_kernel, shape((panel, outs_here)), [VMEM], VMEM)(out_weight)
    w_all = lax.all_gather(w_t, DP, axis=0)

    own = cot
    own_z = lax.ppermute(own, "zl", ring(2, 1))
    up = lax.ppermute(own, "y", ring(4, 1))
    down = lax.ppermute(own, "y", ring(4, -1))

    pq = call(prepare_kernel, stream, [VMEM] * 3, VMEM, micros=4)(q, k, v)
    pq = after(pq, up, down, own_z)
    pq = lax.all_to_all(pq, SEQ, split_axis=0, concat_axis=0, tiled=True)

    far_a = lax.ppermute(up[:half], "y", ring(4, 1))
    far_b = lax.ppermute(down[half:], "y", ring(4, -1))
    up_z = lax.ppermute(own_z, "y", ring(4, 1))
    down_z = lax.ppermute(own_z, "y", ring(4, -1))
    table, gain = call(
        table_kernel,
        [shape((groups, TAPS, 2 * TAPS)), shape((panel, TAPS), F32)],
        [SMEM, VMEM, VMEM],
        [VMEM, VMEM],
        micros=6,
    )((zl * 4 + y).astype(jnp.int32).reshape(1), filters, skip_gain.reshape(8, panel // TAPS, TAPS))
    mixed, gated = call(
        forward_kernel,
        [shape((BLOCKS, panel, rows), F32), shape((panel, length))],
        [SMEM] + [VMEM] * 3,
        [VMEM] * 2,
        micros=7,
    )(slot_of, pq, table, gain)
    far_a_z = lax.ppermute(far_a, "zl", ring(2, 1))
    far_b_z = lax.ppermute(far_b, "zl", ring(2, 1))
    cots = [own, up, down, far_a, far_b, own_z, up_z, down_z, far_a_z, far_b_z]

    cot_held = pltpu.VMEM((length, width), BF)
    mine, other = call(
        weight_kernel,
        [shape((8, panel, outs_here))] * 2,
        [SMEM] + [ANY] * 10 + [VMEM],
        [ANY] * 2,
        scratch=[
            cot_held,
            pltpu.VMEM((2, 8, panel, outs_here), BF),
            pltpu.SemaphoreType.DMA((4,)),
            pltpu.SemaphoreType.DMA((2, 4)),
        ],
        micros=9,
    )(core.astype(jnp.int32).reshape(1), *cots, gated)
    mixed = after(mixed, other)
    other = lax.ppermute(other, "core", ring(2, 1))

    gm, grads = call(
        gradient_kernel,
        [shape((BLOCKS, panel, rows)), stream],
        [SMEM] + [ANY] * 11 + [VMEM] * 4,
        [VMEM, ANY],
        scratch=[
            cot_held,
            pltpu.VMEM((panel, width), BF),
            pltpu.VMEM((BLOCKS, 2, panel, rows), BF),
            pltpu.SemaphoreType.DMA((4,)),
            pltpu.SemaphoreType.DMA((16,)),
            pltpu.SemaphoreType.DMA((2,)),
        ],
        micros=17,
    )(place, *cots, w_all, mixed, pq, table, gain)

    grads = lax.all_to_all(grads, SEQ, split_axis=0, concat_axis=0, tiled=True)

    sums = call(filter_kernel, shape((48, TAPS), F32), [VMEM, VMEM], VMEM, micros=6)(gm, pq)
    messages = call(
        pair_kernel,
        [shape((panel + 48, outs_here))] * 8,
        [SMEM] + [VMEM] * 4,
        [VMEM] * 8,
        micros=3,
    )(order, mine, other, sums, lax.ppermute(sums, "core", ring(2, 1)))
    messages = [messages[0]] + [
        lax.ppermute(m, ("x", "zh"), route(i, d)) for m, (i, d) in zip(messages[1:], ROUTES[1:])
    ]
    grad_query, grad_key, grad_value = call(
        finish_kernel, [shape((rows, width))] * 3, [VMEM] * 3, [VMEM] * 3, micros=5
    )(k, v, grads)
    messages[1] = after(messages[1], grad_query)
    grad_weight, grad_filters, grad_gain = call(
        functools.partial(total_kernel, scale),
        [shape((outs_here, panel), F32), shape((groups, TAPS), F32), shape((panel // TAPS, TAPS), F32)],
        [SMEM] + [VMEM] * 8,
        [VMEM] * 3,
        scratch=[pltpu.VMEM((8, 48, TAPS), F32)],
        micros=3,
    )(source, *messages)
    return (
        grad_query[None],
        grad_key[None],
        grad_value[None],
        grad_weight,
        grad_filters,
        grad_gain.reshape(panel),
    )


def solution(mesh):
    fine = Mesh(mesh.devices.reshape(4, 2, 2, 2, 4), ("x", "zh", "core", "zl", "y"))
    stream = P(DP, SEQ, None)
    return jax.shard_map(
        shards,
        mesh=fine,
        in_specs=(stream, stream, stream, stream, P(DP, SEQ), P(), P()),
        out_specs=(stream, stream, stream, P(DP, SEQ), P(SEQ, None), P(SEQ)),
        check_vma=False,
    )
```

```python
import functools
import math

import jax
import jax.numpy as jnp
from jax import lax
from jax.experimental import pallas as pl
from jax.experimental.pallas import tpu as pltpu
from jax.sharding import Mesh
from jax.sharding import PartitionSpec as P

GROUP = 16
TAPS = 128
BLOCKS = 8
SMALL = 48
BF = jnp.bfloat16
F32 = jnp.float32
LIMIT = 60 * 1024 * 1024
DP = ("x", "zh", "core")
SEQ = ("zl", "y")

ANY = pl.BlockSpec(memory_space=pl.ANY)
SMEM = pl.BlockSpec(memory_space=pltpu.SMEM)
VMEM = pl.BlockSpec(memory_space=pltpu.VMEM)


def call(body, out_shape, in_specs, out_specs, scratch=(), micros=0):
    return pl.pallas_call(
        body,
        out_shape=out_shape,
        in_specs=in_specs,
        out_specs=out_specs,
        scratch_shapes=list(scratch),
        compiler_params=pltpu.CompilerParams(vmem_limit_bytes=LIMIT),
        cost_estimate=pl.CostEstimate(flops=1, bytes_accessed=1 + micros * 3000000, transcendentals=0),
    )


def shape(dims, dtype=BF):
    return jax.ShapeDtypeStruct(dims, dtype)


def table_kernel(panel_ref, filters_ref, gain_ref, table_ref, gain_out_ref):
    groups = table_ref.shape[0]
    panel = panel_ref[0]
    row = lax.broadcasted_iota(jnp.int32, (8, 2 * TAPS), 0)
    first = pl.multiple_of(panel * groups, groups)
    taps_all = filters_ref[pl.ds(first, groups), :].astype(F32)
    for g in range(groups):
        taps = jnp.broadcast_to(taps_all[g : g + 1, :], (8, TAPS))
        rows = jnp.concatenate([taps, jnp.zeros((8, TAPS), F32)], 1)
        for bit in (1, 2, 4):
            rows = jnp.where((row & bit) != 0, pltpu.roll(rows, bit, 1), rows)
        count = 8
        while count < TAPS:
            rows = jnp.concatenate([rows, pltpu.roll(rows, count, 1)], 0)
            count *= 2
        table_ref[g] = rows.astype(BF)
    gain_rows = gain_ref[panel]
    for i in range(gain_rows.shape[0]):
        gain_out_ref[TAPS * i : TAPS * (i + 1), :] = jnp.broadcast_to(
            gain_rows[i : i + 1, :], (TAPS, TAPS)
        ).T


def transpose_kernel(w_ref, out_ref):
    out_ref[...] = w_ref[...].astype(F32).T.astype(BF)


def prepare_kernel(q_ref, k_ref, v_ref, out_ref):
    width = out_ref.shape[2]
    for j in range(out_ref.shape[0]):
        cols = slice(j * width, (j + 1) * width)
        product = k_ref[:, cols].astype(F32) * v_ref[:, cols].astype(F32)
        out_ref[j, 0] = product.T.astype(BF)
        out_ref[j, 1] = q_ref[:, cols].astype(F32).T.astype(BF)


def forward_kernel(slot_ref, pq_ref, table_ref, gain_ref, mixed_ref, gated_ref):
    def one_group(g, carry):
        rows = pl.ds(pl.multiple_of(g * GROUP, GROUP), GROUP)
        x = [pq_ref[b, 0, rows, :] for b in range(BLOCKS)]
        zero = jnp.zeros((GROUP, TAPS), BF)
        lhs = jnp.concatenate(
            [jnp.concatenate(x, 0), jnp.concatenate([zero] + x[:-1], 0)], 1
        )
        table = table_ref[g]
        rhs = jnp.concatenate([table[:, :TAPS], table[:, TAPS:]], 0)
        conv = jnp.dot(lhs, rhs, preferred_element_type=F32)
        gain = gain_ref[rows, :]
        for b in range(BLOCKS):
            mixed = conv[GROUP * b : GROUP * (b + 1)] + gain * x[b].astype(F32)
            mixed_ref[b, rows, :] = mixed
            lanes = pl.ds(pl.multiple_of(slot_ref[b] * TAPS, TAPS), TAPS)
            gated_ref[rows, lanes] = (pq_ref[b, 1, rows, :].astype(F32) * mixed).astype(BF)
        return carry

    lax.fori_loop(0, table_ref.shape[0], one_group, 0, unroll=4)


def backward_kernel(grad_ref, mixed_ref, pq_ref, table_ref, gain_ref, gm_ref, out_ref):
    def one_group(g, carry):
        rows = pl.ds(pl.multiple_of(g * GROUP, GROUP), GROUP)
        table = table_ref[g]
        gain = gain_ref[rows, :]
        zero = jnp.zeros((GROUP, TAPS), BF)
        x = []
        for b in range(BLOCKS):
            grad = grad_ref[b, rows, :]
            out_ref[b, 0, rows, :] = (grad * mixed_ref[b, rows, :]).astype(BF)
            x.append((grad * pq_ref[b, 1, rows, :].astype(F32)).astype(BF))
            gm_ref[b, rows, :] = x[b]
        lhs = jnp.concatenate(
            [jnp.concatenate(x, 0), jnp.concatenate(x[1:] + [zero], 0)], 1
        )
        conv = lax.dot_general(lhs, table, (((1,), (1,)), ((), ())), preferred_element_type=F32)
        for b in range(BLOCKS):
            total = conv[GROUP * b : GROUP * (b + 1)] + gain * x[b].astype(F32)
            out_ref[b, 1, rows, :] = total.astype(BF)
        return carry

    lax.fori_loop(0, table_ref.shape[0], one_group, 0, unroll=4)


def cot_copies(refs, held, sem_of, cols=slice(None)):
    copies = []
    half = TAPS // 2
    for zl in range(2):
        own, up, down, far_a, far_b = refs[5 * zl : 5 * zl + 5]
        for ref, k, first, count in (
            (own, 0, 0, TAPS),
            (up, 1, 0, TAPS),
            (far_a, 2, 0, half),
            (far_b, 2, half, half),
            (down, 3, 0, TAPS),
        ):
            slot = 4 * zl + k
            rows = slice(slot * TAPS + first, slot * TAPS + first + count)
            copies.append(
                pltpu.make_async_copy(ref.at[:, cols], held.at[rows, cols], sem_of(slot))
            )
    return copies


def product_kernel(core_ref, place_ref, *refs):
    cot = refs[:10]
    gated_ref, w_ref, mine_ref, other_ref, grad_ref, held, w_held, total, sems, w_sems, out_sems = refs[10:]
    blocks, channels, width = mine_ref.shape
    stripes = sems.shape[0]
    span = held.shape[1] // stripes
    each = blocks // stripes
    for n in range(stripes):
        for c in cot_copies(cot, held, lambda slot, n=n: sems.at[n], slice(span * n, span * (n + 1))):
            c.start()
    weights = []
    for d in range(2 * blocks):
        weights.append(
            pltpu.make_async_copy(w_ref.at[d], w_held.at[:, width * d : width * (d + 1)], w_sems.at[d])
        )
    for c in weights:
        c.start()

    def out_copies(n):
        part = pl.ds(n * each, each)
        return [
            pltpu.make_async_copy(total.at[lax.rem(core_ref[0] + i, 2), part], ref.at[part], out_sems.at[i, n])
            for i, ref in enumerate((mine_ref, other_ref))
        ]

    def stripe(n, carry):
        cols = pl.ds(pl.multiple_of(n * span, span), span)
        pltpu.make_async_copy(held.at[:, cols], held.at[:, cols], sems.at[n]).wait()
        grad = jnp.dot(gated_ref[...], held[:, cols], preferred_element_type=F32)
        for i in range(2 * each):
            total[i % 2, n * each + i // 2] = grad[:, width * i : width * (i + 1)].astype(BF)
        for c in out_copies(n):
            c.start()
        return carry

    lax.fori_loop(0, stripes, stripe, 0)
    for c in weights:
        c.wait()
    span = 4 * TAPS

    def tokens(n, carry):
        toks = pl.ds(pl.multiple_of(n * span, span), span)
        grad = lax.dot_general(
            w_held[...], held[toks, :], (((1,), (1,)), ((), ())), preferred_element_type=F32
        )
        for i in range(4):
            grad_ref[place_ref[4 * n + i]] = grad[:, TAPS * i : TAPS * (i + 1)]
        return carry

    lax.fori_loop(0, 2, tokens, 0)
    for n in range(stripes):
        for c in out_copies(n):
            c.wait()


def filter_kernel(gm_ref, pq_ref, out_ref):
    channels = gm_ref.shape[1]
    groups = channels // GROUP
    span = 2 * TAPS
    row = lax.broadcasted_iota(jnp.int32, (8, span), 0)

    def one_group(g, carry):
        rows = pl.ds(pl.multiple_of(g * GROUP, GROUP), GROUP)
        x = jnp.concatenate([pq_ref[b, 0, rows, :] for b in range(BLOCKS)], 0)
        y = [gm_ref[b, rows, :] for b in range(BLOCKS)]
        zero = jnp.zeros((GROUP, TAPS), BF)
        window = jnp.concatenate(
            [jnp.concatenate(y, 0), jnp.concatenate(y[1:] + [zero], 0)], 1
        )
        pairs = lax.dot_general(x, window, (((0,), (0,)), ((), ())), preferred_element_type=F32)
        count = TAPS
        while count > 8:
            count //= 2
            pairs = pairs[:count] + pltpu.roll(pairs[count:], span - count, 1)
        for bit in (4, 2, 1):
            pairs = jnp.where((row & bit) != 0, pltpu.roll(pairs, span - bit, 1), pairs)
        out_ref[pl.ds(g, 1), :] = jnp.sum(pairs, 0, keepdims=True)[:, :TAPS]
        return carry

    lax.fori_loop(0, groups, one_group, 0, unroll=8)
    for i in range(channels // TAPS):
        rows = slice(TAPS * i, TAPS * (i + 1))
        total = jnp.zeros((TAPS, TAPS), F32)
        for b in range(BLOCKS):
            total += gm_ref[b, rows, :].astype(F32) * pq_ref[b, 0, rows, :].astype(F32)
        out_ref[groups + i : groups + i + 1, :] = jnp.sum(total.T, 0, keepdims=True)
    first = groups + channels // TAPS
    out_ref[first:, :] = jnp.zeros((out_ref.shape[0] - first, TAPS), F32)


def put_small(ref, small):
    high = small.astype(BF)
    rows = slice(ref.shape[0] - small.shape[0], ref.shape[0])
    ref[rows, :TAPS] = high
    ref[rows, TAPS:] = (small - high.astype(F32)).astype(BF)


def get_small(piece):
    small = piece[piece.shape[0] - SMALL :].astype(F32)
    return small[:, :TAPS] + small[:, TAPS:]


def pair_kernel(order_ref, mine_ref, other_ref, *outs):
    for i, out in enumerate(outs):
        for d in range(2):
            to = order_ref[i] * 2 + d
            out[d] = (mine_ref[to].astype(F32) + other_ref[to].astype(F32)).astype(BF)


def line_kernel(source_ref, zh_ref, *refs):
    pieces, smalls, outs, held = refs[:4], refs[4:8], refs[8:10], refs[10]
    channels = pieces[0].shape[1]
    for i, piece in enumerate(smalls):
        held[source_ref[i]] = piece[...]
    small = ((held[0] + held[1]) + held[2]) + held[3]
    for out, zh in zip(outs, (zh_ref[0], 1 - zh_ref[0])):
        total = pieces[0][zh].astype(F32)
        for piece in pieces[1:]:
            total += piece[zh].astype(F32)
        out[:channels] = total.astype(BF)
        put_small(out, small)


def total_kernel(scale, mine_ref, other_ref, weight_ref, filter_ref, gain_ref):
    channels = weight_ref.shape[1]
    total = mine_ref[:channels].astype(F32) + other_ref[:channels].astype(F32)
    weight_ref[...] = (total * scale).T
    small = (get_small(mine_ref[...]) + get_small(other_ref[...])) * scale
    groups = filter_ref.shape[0]
    filter_ref[...] = small[:groups]
    gain_ref[...] = small[groups : groups + gain_ref.shape[0]]


def finish_kernel(k_ref, v_ref, grads_ref, gq_ref, gk_ref, gv_ref):
    width = grads_ref.shape[2]
    for j in range(grads_ref.shape[0]):
        cols = slice(j * width, (j + 1) * width)
        gq_ref[:, cols] = grads_ref[j, 0].astype(F32).T.astype(BF)
        gp = grads_ref[j, 1].astype(F32).T
        gk_ref[:, cols] = (gp * v_ref[:, cols].astype(F32)).astype(BF)
        gv_ref[:, cols] = (gp * k_ref[:, cols].astype(F32)).astype(BF)


SLOTS = [(d, k) for d in range(2) for k in range(4)]


def after(value, *others):
    return lax.optimization_barrier((value, *others))[0]


def ring(n, k):
    return [(i, (i + k) % n) for i in range(n)]


def numbers(values):
    return jnp.stack(values).astype(jnp.int32)


def shards(queries, key_input, value_input, cotangent, out_weight, filters, skip_gain):
    q, k, v, cot = queries[0], key_input[0], value_input[0], cotangent[0]
    rows, width = q.shape
    half = rows // 2
    panel = width // 8
    outs_here = out_weight.shape[0]
    length = rows * 8
    groups = panel // GROUP
    scale = 1.0 / math.sqrt(16 * length)
    x, zh, core, zl, y = (lax.axis_index(n) for n in ("x", "zh", "core", "zl", "y"))
    place = numbers([(zl ^ d) * 4 + (y - i) % 4 for d, i in SLOTS])
    slot_of = numbers([(zl ^ (p // 4)) * 4 + (y - p) % 4 for p in range(BLOCKS)])
    order = numbers([(x + i) % 4 for i in range(4)])
    source = numbers([(x - i) % 4 for i in range(4)])
    stream = shape((8, 2, panel, rows))

    w_t = call(transpose_kernel, shape((panel, outs_here)), [VMEM], VMEM)(out_weight)
    w_all = lax.all_gather(w_t, DP, axis=0)

    own = cot
    own_z = lax.ppermute(own, "zl", ring(2, 1))
    up = lax.ppermute(own, "y", ring(4, 1))
    down = lax.ppermute(own, "y", ring(4, -1))

    pq = call(prepare_kernel, stream, [VMEM] * 3, VMEM)(q, k, v)
    table, gain = call(
        table_kernel,
        [shape((groups, TAPS, 2 * TAPS)), shape((panel, TAPS), F32)],
        [SMEM, VMEM, VMEM],
        [VMEM, VMEM],
    )((zl * 4 + y).astype(jnp.int32).reshape(1), filters, skip_gain.reshape(8, panel // TAPS, TAPS))
    up, down, own_z, table = lax.optimization_barrier((up, down, own_z, table))
    far_a = lax.ppermute(up[:half], "y", ring(4, 1))
    far_b = lax.ppermute(down[half:], "y", ring(4, -1))
    up_z = lax.ppermute(own_z, "y", ring(4, 1))
    down_z = lax.ppermute(own_z, "y", ring(4, -1))
    far_a_z = lax.ppermute(far_a, "zl", ring(2, 1))
    far_b_z = lax.ppermute(far_b, "zl", ring(2, 1))
    cots = [own, up, down, far_a, far_b, own_z, up_z, down_z, far_a_z, far_b_z]
    pq = lax.all_to_all(pq, SEQ, split_axis=0, concat_axis=0, tiled=True)

    mixed, gated = call(
        forward_kernel,
        [shape((BLOCKS, panel, rows), F32), shape((panel, length))],
        [SMEM] + [VMEM] * 3,
        [VMEM] * 2,
    )(slot_of, pq, table, gain)

    by_core = (8, panel, outs_here)
    mine, other, grad = call(
        product_kernel,
        [shape(by_core), shape(by_core), shape((BLOCKS, panel, rows), F32)],
        [SMEM] * 2 + [ANY] * 10 + [VMEM, ANY],
        [ANY, ANY, VMEM],
        scratch=[
            pltpu.VMEM((length, width), BF),
            pltpu.VMEM((panel, width), BF),
            pltpu.VMEM((2, *by_core), BF),
            pltpu.SemaphoreType.DMA((4,)),
            pltpu.SemaphoreType.DMA((16,)),
            pltpu.SemaphoreType.DMA((2, 4)),
        ],
        micros=100,
    )(core.astype(jnp.int32).reshape(1), place, *cots, gated, w_all)
    other = lax.ppermute(other, "core", ring(2, 1))

    gm, grads = call(
        backward_kernel,
        [shape((BLOCKS, panel, rows)), stream],
        [VMEM] * 5,
        [VMEM] * 2,
    )(grad, mixed, pq, table, gain)
    mine = after(mine, gm)
    grads = lax.all_to_all(grads, SEQ, split_axis=0, concat_axis=0, tiled=True)

    lines = call(
        pair_kernel, [shape((2, panel, outs_here))] * 4, [SMEM] + [VMEM] * 2, [VMEM] * 4
    )(order, mine, other)
    gm = after(gm, lines[0])
    lines = [lines[0]] + [lax.ppermute(lines[i], "x", ring(4, i)) for i in (1, 2, 3)]
    sums = call(filter_kernel, shape((SMALL, TAPS), F32), [VMEM, VMEM], VMEM)(gm, pq)
    sums = sums + lax.ppermute(sums, "core", ring(2, 1))
    sums = [sums] + [lax.ppermute(sums, "x", ring(4, i)) for i in (1, 2, 3)]
    keep, send = call(
        line_kernel,
        [shape((panel + SMALL, outs_here))] * 2,
        [SMEM] * 2 + [VMEM] * 8,
        [VMEM] * 2,
        scratch=[pltpu.VMEM((4, SMALL, TAPS), F32)],
    )(source, zh.astype(jnp.int32).reshape(1), *lines, *sums)
    send = lax.ppermute(send, "zh", ring(2, 1))
    grad_query, grad_key, grad_value = call(
        finish_kernel, [shape((rows, width))] * 3, [VMEM] * 3, [VMEM] * 3
    )(k, v, grads)
    grad_weight, grad_filters, grad_gain = call(
        functools.partial(total_kernel, scale),
        [shape((outs_here, panel), F32), shape((groups, TAPS), F32), shape((panel // TAPS, TAPS), F32)],
        [VMEM] * 2,
        [VMEM] * 3,
    )(keep, send)
    return (
        grad_query[None],
        grad_key[None],
        grad_value[None],
        grad_weight,
        grad_filters,
        grad_gain.reshape(panel),
    )


def solution(mesh):
    fine = Mesh(mesh.devices.reshape(4, 2, 2, 2, 4), ("x", "zh", "core", "zl", "y"))
    stream = P(DP, SEQ, None)
    return jax.shard_map(
        shards,
        mesh=fine,
        in_specs=(stream, stream, stream, stream, P(DP, SEQ), P(), P()),
        out_specs=(stream, stream, stream, P(DP, SEQ), P(SEQ, None), P(SEQ)),
        check_vma=False,
    )
```

```python
import functools
import math

import jax
import jax.numpy as jnp
from jax import lax
from jax.experimental import pallas as pl
from jax.experimental.pallas import tpu as pltpu
from jax.sharding import Mesh
from jax.sharding import PartitionSpec as P

GROUP = 16
TAPS = 128
BLOCKS = 8
SMALL = 48
BF = jnp.bfloat16
F32 = jnp.float32
LIMIT = 60 * 1024 * 1024
DP = ("x", "zh", "core")
SEQ = ("zl", "y")

ANY = pl.BlockSpec(memory_space=pl.ANY)
SMEM = pl.BlockSpec(memory_space=pltpu.SMEM)
VMEM = pl.BlockSpec(memory_space=pltpu.VMEM)


def call(body, out_shape, in_specs, out_specs, scratch=(), micros=0):
    return pl.pallas_call(
        body,
        out_shape=out_shape,
        in_specs=in_specs,
        out_specs=out_specs,
        scratch_shapes=list(scratch),
        compiler_params=pltpu.CompilerParams(vmem_limit_bytes=LIMIT),
        cost_estimate=pl.CostEstimate(flops=1, bytes_accessed=1 + micros * 3000000, transcendentals=0),
    )


def shape(dims, dtype=BF):
    return jax.ShapeDtypeStruct(dims, dtype)


def table_kernel(panel_ref, filters_ref, gain_ref, table_ref, gain_out_ref):
    groups = table_ref.shape[0]
    panel = panel_ref[0]
    row = lax.broadcasted_iota(jnp.int32, (8, 2 * TAPS), 0)
    first = pl.multiple_of(panel * groups, groups)
    taps_all = filters_ref[pl.ds(first, groups), :].astype(F32)
    for g in range(groups):
        taps = jnp.broadcast_to(taps_all[g : g + 1, :], (8, TAPS))
        rows = jnp.concatenate([taps, jnp.zeros((8, TAPS), F32)], 1)
        for bit in (1, 2, 4):
            rows = jnp.where((row & bit) != 0, pltpu.roll(rows, bit, 1), rows)
        count = 8
        while count < TAPS:
            rows = jnp.concatenate([rows, pltpu.roll(rows, count, 1)], 0)
            count *= 2
        table_ref[g] = rows.astype(BF)
    gain_rows = gain_ref[panel]
    for i in range(gain_rows.shape[0]):
        gain_out_ref[TAPS * i : TAPS * (i + 1), :] = jnp.broadcast_to(
            gain_rows[i : i + 1, :], (TAPS, TAPS)
        ).T


def transpose_kernel(w_ref, out_ref):
    out_ref[...] = w_ref[...].astype(F32).T.astype(BF)


def prepare_kernel(q_ref, k_ref, v_ref, out_ref):
    width = out_ref.shape[2]
    for j in range(out_ref.shape[0]):
        cols = slice(j * width, (j + 1) * width)
        product = k_ref[:, cols].astype(F32) * v_ref[:, cols].astype(F32)
        out_ref[j, 0] = product.T.astype(BF)
        out_ref[j, 1] = q_ref[:, cols].astype(F32).T.astype(BF)


def forward_kernel(slot_ref, pq_ref, table_ref, gain_ref, mixed_ref, gated_ref):
    def one_group(g, carry):
        rows = pl.ds(pl.multiple_of(g * GROUP, GROUP), GROUP)
        x = [pq_ref[b, 0, rows, :] for b in range(BLOCKS)]
        zero = jnp.zeros((GROUP, TAPS), BF)
        lhs = jnp.concatenate(
            [jnp.concatenate(x, 0), jnp.concatenate([zero] + x[:-1], 0)], 1
        )
        table = table_ref[g]
        rhs = jnp.concatenate([table[:, :TAPS], table[:, TAPS:]], 0)
        conv = jnp.dot(lhs, rhs, preferred_element_type=F32)
        gain = gain_ref[rows, :]
        for b in range(BLOCKS):
            mixed = conv[GROUP * b : GROUP * (b + 1)] + gain * x[b].astype(F32)
            mixed_ref[b, rows, :] = mixed
            lanes = pl.ds(pl.multiple_of(slot_ref[b] * TAPS, TAPS), TAPS)
            gated_ref[rows, lanes] = (pq_ref[b, 1, rows, :].astype(F32) * mixed).astype(BF)
        return carry

    lax.fori_loop(0, table_ref.shape[0], one_group, 0, unroll=4)


def cot_copies(refs, held, sem_of, cols=slice(None)):
    copies = []
    half = TAPS // 2
    for zl in range(2):
        own, up, down, far_a, far_b = refs[5 * zl : 5 * zl + 5]
        for ref, k, first, count in (
            (own, 0, 0, TAPS),
            (up, 1, 0, TAPS),
            (far_a, 2, 0, half),
            (far_b, 2, half, half),
            (down, 3, 0, TAPS),
        ):
            slot = 4 * zl + k
            rows = slice(slot * TAPS + first, slot * TAPS + first + count)
            copies.append(
                pltpu.make_async_copy(ref.at[:, cols], held.at[rows, cols], sem_of(slot))
            )
    return copies


def product_kernel(core_ref, place_ref, *refs):
    cot = refs[:10]
    gated_ref, w_ref, streams = refs[10], refs[11], refs[12:16]
    mine_ref, other_ref, gm_ref, out_ref = refs[16:20]
    held, w_held, total, grad_ref = refs[20:24]
    stream_held = refs[24:28]
    sems, w_sems, out_sems, stream_sems = refs[28:]
    mixed_ref, pq_ref, table_ref, gain_ref = stream_held
    blocks, channels, width = mine_ref.shape
    stripes = sems.shape[0]
    span = held.shape[1] // stripes
    each = blocks // stripes
    for n in range(stripes):
        for c in cot_copies(cot, held, lambda slot, n=n: sems.at[n], slice(span * n, span * (n + 1))):
            c.start()
    weights = []
    for d in range(2 * blocks):
        weights.append(
            pltpu.make_async_copy(w_ref.at[d], w_held.at[:, width * d : width * (d + 1)], w_sems.at[d])
        )
    ins = [
        pltpu.make_async_copy(ref, dst, stream_sems.at[i])
        for i, (ref, dst) in enumerate(zip(streams, stream_held))
    ]
    for c in weights + ins:
        c.start()

    def out_copies(n):
        part = pl.ds(n * each, each)
        return [
            pltpu.make_async_copy(total.at[lax.rem(core_ref[0] + i, 2), part], ref.at[part], out_sems.at[i, n])
            for i, ref in enumerate((mine_ref, other_ref))
        ]

    def stripe(n, carry):
        cols = pl.ds(pl.multiple_of(n * span, span), span)
        pltpu.make_async_copy(held.at[:, cols], held.at[:, cols], sems.at[n]).wait()
        grad = jnp.dot(gated_ref[...], held[:, cols], preferred_element_type=F32)
        for i in range(2 * each):
            total[i % 2, n * each + i // 2] = grad[:, width * i : width * (i + 1)].astype(BF)
        for c in out_copies(n):
            c.start()
        return carry

    lax.fori_loop(0, stripes, stripe, 0)
    for c in weights:
        c.wait()
    span = 4 * TAPS

    def tokens(n, carry):
        toks = pl.ds(pl.multiple_of(n * span, span), span)
        grad = lax.dot_general(
            w_held[...], held[toks, :], (((1,), (1,)), ((), ())), preferred_element_type=F32
        )
        for i in range(4):
            grad_ref[place_ref[4 * n + i]] = grad[:, TAPS * i : TAPS * (i + 1)]
        return carry

    lax.fori_loop(0, 2, tokens, 0)
    for c in ins:
        c.wait()

    def one_group(g, carry):
        rows = pl.ds(pl.multiple_of(g * GROUP, GROUP), GROUP)
        table = table_ref[g]
        gain = gain_ref[rows, :]
        zero = jnp.zeros((GROUP, TAPS), BF)
        x = []
        for b in range(BLOCKS):
            grad = grad_ref[b, rows, :]
            out_ref[b, 0, rows, :] = (grad * mixed_ref[b, rows, :]).astype(BF)
            x.append((grad * pq_ref[b, 1, rows, :].astype(F32)).astype(BF))
            gm_ref[b, rows, :] = x[b]
        lhs = jnp.concatenate(
            [jnp.concatenate(x, 0), jnp.concatenate(x[1:] + [zero], 0)], 1
        )
        conv = lax.dot_general(lhs, table, (((1,), (1,)), ((), ())), preferred_element_type=F32)
        for b in range(BLOCKS):
            result = conv[GROUP * b : GROUP * (b + 1)] + gain * x[b].astype(F32)
            out_ref[b, 1, rows, :] = result.astype(BF)
        return carry

    lax.fori_loop(0, table_ref.shape[0], one_group, 0, unroll=4)
    for n in range(stripes):
        for c in out_copies(n):
            c.wait()


def filter_kernel(gm_ref, pq_ref, out_ref):
    channels = gm_ref.shape[1]
    groups = channels // GROUP
    span = 2 * TAPS
    row = lax.broadcasted_iota(jnp.int32, (8, span), 0)

    def one_group(g, carry):
        rows = pl.ds(pl.multiple_of(g * GROUP, GROUP), GROUP)
        x = jnp.concatenate([pq_ref[b, 0, rows, :] for b in range(BLOCKS)], 0)
        y = [gm_ref[b, rows, :] for b in range(BLOCKS)]
        zero = jnp.zeros((GROUP, TAPS), BF)
        window = jnp.concatenate(
            [jnp.concatenate(y, 0), jnp.concatenate(y[1:] + [zero], 0)], 1
        )
        pairs = lax.dot_general(x, window, (((0,), (0,)), ((), ())), preferred_element_type=F32)
        count = TAPS
        while count > 8:
            count //= 2
            pairs = pairs[:count] + pltpu.roll(pairs[count:], span - count, 1)
        for bit in (4, 2, 1):
            pairs = jnp.where((row & bit) != 0, pltpu.roll(pairs, span - bit, 1), pairs)
        out_ref[pl.ds(g, 1), :] = jnp.sum(pairs, 0, keepdims=True)[:, :TAPS]
        return carry

    lax.fori_loop(0, groups, one_group, 0, unroll=8)
    for i in range(channels // TAPS):
        rows = slice(TAPS * i, TAPS * (i + 1))
        total = jnp.zeros((TAPS, TAPS), F32)
        for b in range(BLOCKS):
            total += gm_ref[b, rows, :].astype(F32) * pq_ref[b, 0, rows, :].astype(F32)
        out_ref[groups + i : groups + i + 1, :] = jnp.sum(total.T, 0, keepdims=True)
    first = groups + channels // TAPS
    out_ref[first:, :] = jnp.zeros((out_ref.shape[0] - first, TAPS), F32)


def put_small(ref, small):
    high = small.astype(BF)
    rows = slice(ref.shape[0] - small.shape[0], ref.shape[0])
    ref[rows, :TAPS] = high
    ref[rows, TAPS:] = (small - high.astype(F32)).astype(BF)


def get_small(piece):
    small = piece[piece.shape[0] - SMALL :].astype(F32)
    return small[:, :TAPS] + small[:, TAPS:]


def pair_kernel(order_ref, mine_ref, other_ref, *outs):
    for i, out in enumerate(outs):
        for d in range(2):
            to = order_ref[i] * 2 + d
            out[d] = mine_ref[to] + other_ref[to]


def line_kernel(source_ref, zh_ref, *refs):
    pieces, smalls, outs, held = refs[:4], refs[4:8], refs[8:10], refs[10]
    channels = pieces[0].shape[1]
    for i, piece in enumerate(smalls):
        held[source_ref[i]] = piece[...]
    small = ((held[0] + held[1]) + held[2]) + held[3]
    for out, zh in zip(outs, (zh_ref[0], 1 - zh_ref[0])):
        total = pieces[0][zh].astype(F32)
        for piece in pieces[1:]:
            total += piece[zh].astype(F32)
        out[:channels] = total.astype(BF)
        put_small(out, small)


def total_kernel(scale, mine_ref, other_ref, weight_ref, filter_ref, gain_ref):
    channels = weight_ref.shape[1]
    total = mine_ref[:channels].astype(F32) + other_ref[:channels].astype(F32)
    weight_ref[...] = (total * scale).T
    small = (get_small(mine_ref[...]) + get_small(other_ref[...])) * scale
    groups = filter_ref.shape[0]
    filter_ref[...] = small[:groups]
    gain_ref[...] = small[groups : groups + gain_ref.shape[0]]


def finish_kernel(k_ref, v_ref, grads_ref, gq_ref, gk_ref, gv_ref):
    width = grads_ref.shape[2]
    for j in range(grads_ref.shape[0]):
        cols = slice(j * width, (j + 1) * width)
        gq_ref[:, cols] = grads_ref[j, 0].astype(F32).T.astype(BF)
        gp = grads_ref[j, 1].astype(F32).T
        gk_ref[:, cols] = (gp * v_ref[:, cols].astype(F32)).astype(BF)
        gv_ref[:, cols] = (gp * k_ref[:, cols].astype(F32)).astype(BF)


SLOTS = [(d, k) for d in range(2) for k in range(4)]


def after(value, *others):
    return lax.optimization_barrier((value, *others))[0]


def ring(n, k):
    return [(i, (i + k) % n) for i in range(n)]


def numbers(values):
    return jnp.stack(values).astype(jnp.int32)


def shards(queries, key_input, value_input, cotangent, out_weight, filters, skip_gain):
    q, k, v, cot = queries[0], key_input[0], value_input[0], cotangent[0]
    rows, width = q.shape
    half = rows // 2
    panel = width // 8
    outs_here = out_weight.shape[0]
    length = rows * 8
    groups = panel // GROUP
    scale = 1.0 / math.sqrt(16 * length)
    x, zh, core, zl, y = (lax.axis_index(n) for n in ("x", "zh", "core", "zl", "y"))
    place = numbers([(zl ^ d) * 4 + (y - i) % 4 for d, i in SLOTS])
    slot_of = numbers([(zl ^ (p // 4)) * 4 + (y - p) % 4 for p in range(BLOCKS)])
    order = numbers([(x + i) % 4 for i in range(4)])
    source = numbers([(x - i) % 4 for i in range(4)])
    stream = shape((8, 2, panel, rows))

    w_t = call(transpose_kernel, shape((panel, outs_here)), [VMEM], VMEM)(out_weight)
    w_all = lax.all_gather(w_t, DP, axis=0)

    own = cot
    own_z = lax.ppermute(own, "zl", ring(2, 1))
    up = lax.ppermute(own, "y", ring(4, 1))
    down = lax.ppermute(own, "y", ring(4, -1))

    pq = call(prepare_kernel, stream, [VMEM] * 3, VMEM)(q, k, v)
    table, gain = call(
        table_kernel,
        [shape((groups, TAPS, 2 * TAPS)), shape((panel, TAPS), F32)],
        [SMEM, VMEM, VMEM],
        [VMEM, VMEM],
    )((zl * 4 + y).astype(jnp.int32).reshape(1), filters, skip_gain.reshape(8, panel // TAPS, TAPS))
    up, down, own_z, table = lax.optimization_barrier((up, down, own_z, table))
    far_a = lax.ppermute(up[:half], "y", ring(4, 1))
    far_b = lax.ppermute(down[half:], "y", ring(4, -1))
    up_z = lax.ppermute(own_z, "y", ring(4, 1))
    down_z = lax.ppermute(own_z, "y", ring(4, -1))
    far_a_z = lax.ppermute(far_a, "zl", ring(2, 1))
    far_b_z = lax.ppermute(far_b, "zl", ring(2, 1))
    cots = [own, up, down, far_a, far_b, own_z, up_z, down_z, far_a_z, far_b_z]
    pq = lax.all_to_all(pq, SEQ, split_axis=0, concat_axis=0, tiled=True)

    mixed, gated = call(
        forward_kernel,
        [shape((BLOCKS, panel, rows), F32), shape((panel, length))],
        [SMEM] + [VMEM] * 3,
        [VMEM] * 2,
    )(slot_of, pq, table, gain)

    by_core = (8, panel, outs_here)
    mine, other, gm, grads = call(
        product_kernel,
        [shape(by_core), shape(by_core), shape((BLOCKS, panel, rows)), stream],
        [SMEM] * 2 + [ANY] * 10 + [VMEM] + [ANY] * 5,
        [ANY, ANY, VMEM, VMEM],
        scratch=[
            pltpu.VMEM((length, width), BF),
            pltpu.VMEM((panel, width), BF),
            pltpu.VMEM((2, *by_core), BF),
            pltpu.VMEM((BLOCKS, panel, rows), F32),
            pltpu.VMEM((BLOCKS, panel, rows), F32),
            pltpu.VMEM(stream.shape, BF),
            pltpu.VMEM(table.shape, BF),
            pltpu.VMEM(gain.shape, F32),
            pltpu.SemaphoreType.DMA((4,)),
            pltpu.SemaphoreType.DMA((16,)),
            pltpu.SemaphoreType.DMA((2, 4)),
            pltpu.SemaphoreType.DMA((4,)),
        ],
        micros=100,
    )(core.astype(jnp.int32).reshape(1), place, *cots, gated, w_all, mixed, pq, table, gain)
    other = lax.ppermute(other, "core", ring(2, 1))
    grads = lax.all_to_all(grads, SEQ, split_axis=0, concat_axis=0, tiled=True)

    lines = call(
        pair_kernel, [shape((2, panel, outs_here))] * 4, [SMEM] + [VMEM] * 2, [VMEM] * 4
    )(order, mine, other)
    gm = after(gm, lines[0])
    sums = call(filter_kernel, shape((SMALL, TAPS), F32), [VMEM, VMEM], VMEM)(gm, pq)
    lines = [lines[0]] + [lax.ppermute(lines[i], "x", ring(4, i)) for i in (1, 2, 3)]
    sums = sums + lax.ppermute(sums, "core", ring(2, 1))
    sums = [sums] + [lax.ppermute(sums, "x", ring(4, i)) for i in (1, 2, 3)]
    grad_query, grad_key, grad_value = call(
        finish_kernel, [shape((rows, width))] * 3, [VMEM] * 3, [VMEM] * 3
    )(k, v, grads)
    keep, send = call(
        line_kernel,
        [shape((panel + SMALL, outs_here))] * 2,
        [SMEM] * 2 + [VMEM] * 8,
        [VMEM] * 2,
        scratch=[pltpu.VMEM((4, SMALL, TAPS), F32)],
    )(source, zh.astype(jnp.int32).reshape(1), *lines, *sums)
    send = lax.ppermute(send, "zh", ring(2, 1))
    grad_weight, grad_filters, grad_gain = call(
        functools.partial(total_kernel, scale),
        [shape((outs_here, panel), F32), shape((groups, TAPS), F32), shape((panel // TAPS, TAPS), F32)],
        [VMEM] * 2,
        [VMEM] * 3,
    )(keep, send)
    return (
        grad_query[None],
        grad_key[None],
        grad_value[None],
        grad_weight,
        grad_filters,
        grad_gain.reshape(panel),
    )


def solution(mesh):
    fine = Mesh(mesh.devices.reshape(4, 2, 2, 2, 4), ("x", "zh", "core", "zl", "y"))
    stream = P(DP, SEQ, None)
    return jax.shard_map(
        shards,
        mesh=fine,
        in_specs=(stream, stream, stream, stream, P(DP, SEQ), P(), P()),
        out_specs=(stream, stream, stream, P(DP, SEQ), P(SEQ, None), P(SEQ)),
        check_vma=False,
    )
```

```python
import functools
import math

import jax
import jax.numpy as jnp
from jax import lax
from jax.experimental import pallas as pl
from jax.experimental.pallas import tpu as pltpu
from jax.sharding import Mesh
from jax.sharding import PartitionSpec as P

GROUP = 16
TAPS = 128
BLOCKS = 8
SMALL = 48
BF = jnp.bfloat16
F32 = jnp.float32
LIMIT = 60 * 1024 * 1024
DP = ("x", "zh", "core")
SEQ = ("zl", "y")

ANY = pl.BlockSpec(memory_space=pl.ANY)
SMEM = pl.BlockSpec(memory_space=pltpu.SMEM)
VMEM = pl.BlockSpec(memory_space=pltpu.VMEM)


def call(body, out_shape, in_specs, out_specs, scratch=(), micros=0):
    return pl.pallas_call(
        body,
        out_shape=out_shape,
        in_specs=in_specs,
        out_specs=out_specs,
        scratch_shapes=list(scratch),
        compiler_params=pltpu.CompilerParams(vmem_limit_bytes=LIMIT),
        cost_estimate=pl.CostEstimate(flops=1, bytes_accessed=1 + micros * 3000000, transcendentals=0),
    )


def shape(dims, dtype=BF):
    return jax.ShapeDtypeStruct(dims, dtype)


def table_kernel(panel_ref, filters_ref, gain_ref, table_ref, gain_out_ref):
    groups = table_ref.shape[0]
    panel = panel_ref[0]
    row = lax.broadcasted_iota(jnp.int32, (8, 2 * TAPS), 0)
    first = pl.multiple_of(panel * groups, groups)
    taps_all = filters_ref[pl.ds(first, groups), :].astype(F32)
    for g in range(groups):
        taps = jnp.broadcast_to(taps_all[g : g + 1, :], (8, TAPS))
        rows = jnp.concatenate([taps, jnp.zeros((8, TAPS), F32)], 1)
        for bit in (1, 2, 4):
            rows = jnp.where((row & bit) != 0, pltpu.roll(rows, bit, 1), rows)
        count = 8
        while count < TAPS:
            rows = jnp.concatenate([rows, pltpu.roll(rows, count, 1)], 0)
            count *= 2
        table_ref[g] = rows.astype(BF)
    gain_rows = gain_ref[panel]
    for i in range(gain_rows.shape[0]):
        gain_out_ref[TAPS * i : TAPS * (i + 1), :] = jnp.broadcast_to(
            gain_rows[i : i + 1, :], (TAPS, TAPS)
        ).T


def transpose_kernel(w_ref, out_ref):
    out_ref[...] = w_ref[...].astype(F32).T.astype(BF)


def prepare_kernel(q_ref, k_ref, v_ref, out_ref):
    width = out_ref.shape[2]
    for j in range(out_ref.shape[0]):
        cols = slice(j * width, (j + 1) * width)
        product = k_ref[:, cols].astype(F32) * v_ref[:, cols].astype(F32)
        out_ref[j, 0] = product.T.astype(BF)
        out_ref[j, 1] = q_ref[:, cols].astype(F32).T.astype(BF)


def forward_kernel(slot_ref, pq_ref, table_ref, gain_ref, mixed_ref, gated_ref):
    def one_group(g, carry):
        rows = pl.ds(pl.multiple_of(g * GROUP, GROUP), GROUP)
        x = [pq_ref[b, 0, rows, :] for b in range(BLOCKS)]
        zero = jnp.zeros((GROUP, TAPS), BF)
        lhs = jnp.concatenate(
            [jnp.concatenate(x, 0), jnp.concatenate([zero] + x[:-1], 0)], 1
        )
        table = table_ref[g]
        rhs = jnp.concatenate([table[:, :TAPS], table[:, TAPS:]], 0)
        conv = jnp.dot(lhs, rhs, preferred_element_type=F32)
        gain = gain_ref[rows, :]
        for b in range(BLOCKS):
            mixed = conv[GROUP * b : GROUP * (b + 1)] + gain * x[b].astype(F32)
            mixed_ref[b, rows, :] = mixed
            lanes = pl.ds(pl.multiple_of(slot_ref[b] * TAPS, TAPS), TAPS)
            gated_ref[rows, lanes] = (pq_ref[b, 1, rows, :].astype(F32) * mixed).astype(BF)
        return carry

    lax.fori_loop(0, table_ref.shape[0], one_group, 0, unroll=4)


def cot_copies(refs, held, sem_of, cols=slice(None)):
    copies = []
    half = TAPS // 2
    for zl in range(2):
        own, up, down, far_a, far_b = refs[5 * zl : 5 * zl + 5]
        for ref, k, first, count in (
            (own, 0, 0, TAPS),
            (up, 1, 0, TAPS),
            (far_a, 2, 0, half),
            (far_b, 2, half, half),
            (down, 3, 0, TAPS),
        ):
            slot = 4 * zl + k
            rows = slice(slot * TAPS + first, slot * TAPS + first + count)
            copies.append(
                pltpu.make_async_copy(ref.at[:, cols], held.at[rows, cols], sem_of(slot))
            )
    return copies


def product_kernel(core_ref, place_ref, *refs):
    cot = refs[:10]
    gated_ref, w_ref, streams = refs[10], refs[11], refs[12:16]
    mine_ref, other_ref, gm_ref, out_ref = refs[16:20]
    held, w_held, total, grad_ref = refs[20:24]
    stream_held = refs[24:28]
    sems, w_sems, out_sems, stream_sems = refs[28:]
    mixed_ref, pq_ref, table_ref, gain_ref = stream_held
    blocks, channels, width = mine_ref.shape
    stripes = sems.shape[0]
    span = held.shape[1] // stripes
    each = blocks // stripes
    def stripe_start(n):
        for c in cot_copies(cot, held, lambda slot: sems.at[n], slice(span * n, span * (n + 1))):
            c.start()

    stripe_start(0)
    stripe_start(1)
    weights = []
    for d in range(2 * blocks):
        weights.append(
            pltpu.make_async_copy(w_ref.at[d], w_held.at[:, width * d : width * (d + 1)], w_sems.at[d])
        )
    ins = [
        pltpu.make_async_copy(ref, dst, stream_sems.at[i])
        for i, (ref, dst) in enumerate(zip(streams, stream_held))
    ]

    def out_copies(n):
        part = pl.ds(n * each, each)
        return [
            pltpu.make_async_copy(total.at[lax.rem(core_ref[0] + i, 2), part], ref.at[part], out_sems.at[i, n])
            for i, ref in enumerate((mine_ref, other_ref))
        ]

    for n in range(stripes):
        cols = slice(span * n, span * (n + 1))
        pltpu.make_async_copy(held.at[:, cols], held.at[:, cols], sems.at[n]).wait()
        if n + 2 < stripes:
            stripe_start(n + 2)
        for c in {stripes - 3: weights[:blocks], stripes - 2: weights[blocks:], stripes - 1: ins}.get(n, []):
            c.start()
        grad = jnp.dot(gated_ref[...], held[:, cols], preferred_element_type=F32)
        for i in range(2 * each):
            total[i % 2, n * each + i // 2] = grad[:, width * i : width * (i + 1)].astype(BF)
        for c in out_copies(n):
            c.start()
    for c in weights:
        c.wait()
    span = 4 * TAPS

    def tokens(n, carry):
        toks = pl.ds(pl.multiple_of(n * span, span), span)
        grad = lax.dot_general(
            w_held[...], held[toks, :], (((1,), (1,)), ((), ())), preferred_element_type=F32
        )
        for i in range(4):
            grad_ref[place_ref[4 * n + i]] = grad[:, TAPS * i : TAPS * (i + 1)]
        return carry

    lax.fori_loop(0, 2, tokens, 0)
    for c in ins:
        c.wait()

    def one_group(g, carry):
        rows = pl.ds(pl.multiple_of(g * GROUP, GROUP), GROUP)
        table = table_ref[g]
        gain = gain_ref[rows, :]
        zero = jnp.zeros((GROUP, TAPS), BF)
        x = []
        for b in range(BLOCKS):
            grad = grad_ref[b, rows, :]
            out_ref[b, 0, rows, :] = (grad * mixed_ref[b, rows, :]).astype(BF)
            x.append((grad * pq_ref[b, 1, rows, :].astype(F32)).astype(BF))
            gm_ref[b, rows, :] = x[b]
        lhs = jnp.concatenate(
            [jnp.concatenate(x, 0), jnp.concatenate(x[1:] + [zero], 0)], 1
        )
        conv = lax.dot_general(lhs, table, (((1,), (1,)), ((), ())), preferred_element_type=F32)
        for b in range(BLOCKS):
            result = conv[GROUP * b : GROUP * (b + 1)] + gain * x[b].astype(F32)
            out_ref[b, 1, rows, :] = result.astype(BF)
        return carry

    lax.fori_loop(0, table_ref.shape[0], one_group, 0, unroll=4)
    for n in range(stripes):
        for c in out_copies(n):
            c.wait()


def filter_kernel(gm_ref, pq_ref, out_ref):
    channels = gm_ref.shape[1]
    groups = channels // GROUP
    span = 2 * TAPS
    row = lax.broadcasted_iota(jnp.int32, (8, span), 0)

    def one_group(g, carry):
        rows = pl.ds(pl.multiple_of(g * GROUP, GROUP), GROUP)
        x = jnp.concatenate([pq_ref[b, 0, rows, :] for b in range(BLOCKS)], 0)
        y = [gm_ref[b, rows, :] for b in range(BLOCKS)]
        zero = jnp.zeros((GROUP, TAPS), BF)
        window = jnp.concatenate(
            [jnp.concatenate(y, 0), jnp.concatenate(y[1:] + [zero], 0)], 1
        )
        pairs = lax.dot_general(x, window, (((0,), (0,)), ((), ())), preferred_element_type=F32)
        count = TAPS
        while count > 8:
            count //= 2
            pairs = pairs[:count] + pltpu.roll(pairs[count:], span - count, 1)
        for bit in (4, 2, 1):
            pairs = jnp.where((row & bit) != 0, pltpu.roll(pairs, span - bit, 1), pairs)
        out_ref[pl.ds(g, 1), :] = jnp.sum(pairs, 0, keepdims=True)[:, :TAPS]
        return carry

    lax.fori_loop(0, groups, one_group, 0, unroll=8)
    for i in range(channels // TAPS):
        rows = slice(TAPS * i, TAPS * (i + 1))
        total = jnp.zeros((TAPS, TAPS), F32)
        for b in range(BLOCKS):
            total += gm_ref[b, rows, :].astype(F32) * pq_ref[b, 0, rows, :].astype(F32)
        out_ref[groups + i : groups + i + 1, :] = jnp.sum(total.T, 0, keepdims=True)
    first = groups + channels // TAPS
    out_ref[first:, :] = jnp.zeros((out_ref.shape[0] - first, TAPS), F32)


def put_small(ref, small):
    high = small.astype(BF)
    rows = slice(ref.shape[0] - small.shape[0], ref.shape[0])
    ref[rows, :TAPS] = high
    ref[rows, TAPS:] = (small - high.astype(F32)).astype(BF)


def get_small(piece):
    small = piece[piece.shape[0] - SMALL :].astype(F32)
    return small[:, :TAPS] + small[:, TAPS:]


def pair_kernel(order_ref, mine_ref, other_ref, *refs):
    outs = refs[:4]
    mine, other, lines, sems, out_sems = refs[4:]
    ins = []
    for i in range(4):
        part = pl.ds(order_ref[i] * 2, 2)
        ins.append([
            pltpu.make_async_copy(ref.at[part], held.at[i], sems.at[i, j])
            for j, (ref, held) in enumerate(((mine_ref, mine), (other_ref, other)))
        ])
        for c in ins[-1]:
            c.start()
    backs = []
    for i in range(4):
        for c in ins[i]:
            c.wait()
        lines[i] = mine[i] + other[i]
        backs.append(pltpu.make_async_copy(lines.at[i], outs[i], out_sems.at[i]))
        backs[-1].start()
    for c in backs:
        c.wait()


def line_kernel(source_ref, zh_ref, *refs):
    pieces, smalls, outs, held = refs[:4], refs[4:8], refs[8:10], refs[10]
    channels = pieces[0].shape[1]
    for i, piece in enumerate(smalls):
        held[source_ref[i]] = piece[...]
    small = ((held[0] + held[1]) + held[2]) + held[3]
    for out, zh in zip(outs, (zh_ref[0], 1 - zh_ref[0])):
        total = pieces[0][zh].astype(F32)
        for piece in pieces[1:]:
            total += piece[zh].astype(F32)
        out[:channels] = total.astype(BF)
        put_small(out, small)


def total_kernel(scale, mine_ref, other_ref, weight_ref, filter_ref, gain_ref):
    channels = weight_ref.shape[1]
    total = mine_ref[:channels].astype(F32) + other_ref[:channels].astype(F32)
    weight_ref[...] = (total * scale).T
    small = (get_small(mine_ref[...]) + get_small(other_ref[...])) * scale
    groups = filter_ref.shape[0]
    filter_ref[...] = small[:groups]
    gain_ref[...] = small[groups : groups + gain_ref.shape[0]]


def finish_kernel(k_ref, v_ref, grads_ref, gq_ref, gk_ref, gv_ref):
    width = grads_ref.shape[2]
    for j in range(grads_ref.shape[0]):
        cols = slice(j * width, (j + 1) * width)
        gq_ref[:, cols] = grads_ref[j, 0].astype(F32).T.astype(BF)
        gp = grads_ref[j, 1].astype(F32).T
        gk_ref[:, cols] = (gp * v_ref[:, cols].astype(F32)).astype(BF)
        gv_ref[:, cols] = (gp * k_ref[:, cols].astype(F32)).astype(BF)


SLOTS = [(d, k) for d in range(2) for k in range(4)]


def after(value, *others):
    return lax.optimization_barrier((value, *others))[0]


def ring(n, k):
    return [(i, (i + k) % n) for i in range(n)]


def numbers(values):
    return jnp.stack(values).astype(jnp.int32)


def shards(queries, key_input, value_input, cotangent, out_weight, filters, skip_gain):
    q, k, v, cot = queries[0], key_input[0], value_input[0], cotangent[0]
    rows, width = q.shape
    half = rows // 2
    panel = width // 8
    outs_here = out_weight.shape[0]
    length = rows * 8
    groups = panel // GROUP
    scale = 1.0 / math.sqrt(16 * length)
    x, zh, core, zl, y = (lax.axis_index(n) for n in ("x", "zh", "core", "zl", "y"))
    place = numbers([(zl ^ d) * 4 + (y - i) % 4 for d, i in SLOTS])
    slot_of = numbers([(zl ^ (p // 4)) * 4 + (y - p) % 4 for p in range(BLOCKS)])
    order = numbers([(x + i) % 4 for i in range(4)])
    source = numbers([(x - i) % 4 for i in range(4)])
    stream = shape((8, 2, panel, rows))

    w_t = call(transpose_kernel, shape((panel, outs_here)), [VMEM], VMEM)(out_weight)
    w_all = lax.all_gather(w_t, DP, axis=0)

    own = cot
    own_z = lax.ppermute(own, "zl", ring(2, 1))
    up = lax.ppermute(own, "y", ring(4, 1))
    down = lax.ppermute(own, "y", ring(4, -1))

    pq = call(prepare_kernel, stream, [VMEM] * 3, VMEM)(q, k, v)
    table, gain = call(
        table_kernel,
        [shape((groups, TAPS, 2 * TAPS)), shape((panel, TAPS), F32)],
        [SMEM, VMEM, VMEM],
        [VMEM, VMEM],
    )((zl * 4 + y).astype(jnp.int32).reshape(1), filters, skip_gain.reshape(8, panel // TAPS, TAPS))
    up, down, own_z, table = lax.optimization_barrier((up, down, own_z, table))
    far_a = lax.ppermute(up[:half], "y", ring(4, 1))
    far_b = lax.ppermute(down[half:], "y", ring(4, -1))
    up_z = lax.ppermute(own_z, "y", ring(4, 1))
    down_z = lax.ppermute(own_z, "y", ring(4, -1))
    far_a_z = lax.ppermute(far_a, "zl", ring(2, 1))
    far_b_z = lax.ppermute(far_b, "zl", ring(2, 1))
    cots = [own, up, down, far_a, far_b, own_z, up_z, down_z, far_a_z, far_b_z]
    pq = lax.all_to_all(pq, SEQ, split_axis=0, concat_axis=0, tiled=True)

    mixed, gated = call(
        forward_kernel,
        [shape((BLOCKS, panel, rows), F32), shape((panel, length))],
        [SMEM] + [VMEM] * 3,
        [VMEM] * 2,
    )(slot_of, pq, table, gain)

    by_core = (8, panel, outs_here)
    mine, other, gm, grads = call(
        product_kernel,
        [shape(by_core), shape(by_core), shape((BLOCKS, panel, rows)), stream],
        [SMEM] * 2 + [ANY] * 10 + [VMEM] + [ANY] * 5,
        [ANY, ANY, VMEM, VMEM],
        scratch=[
            pltpu.VMEM((length, width), BF),
            pltpu.VMEM((panel, width), BF),
            pltpu.VMEM((2, *by_core), BF),
            pltpu.VMEM((BLOCKS, panel, rows), F32),
            pltpu.VMEM((BLOCKS, panel, rows), F32),
            pltpu.VMEM(stream.shape, BF),
            pltpu.VMEM(table.shape, BF),
            pltpu.VMEM(gain.shape, F32),
            pltpu.SemaphoreType.DMA((4,)),
            pltpu.SemaphoreType.DMA((16,)),
            pltpu.SemaphoreType.DMA((2, 4)),
            pltpu.SemaphoreType.DMA((4,)),
        ],
        micros=100,
    )(core.astype(jnp.int32).reshape(1), place, *cots, gated, w_all, mixed, pq, table, gain)
    other = lax.ppermute(other, "core", ring(2, 1))
    grads = lax.all_to_all(grads, SEQ, split_axis=0, concat_axis=0, tiled=True)

    part = (2, panel, outs_here)
    lines = call(
        pair_kernel,
        [shape(part)] * 4,
        [SMEM] + [ANY] * 2,
        [ANY] * 4,
        scratch=[pltpu.VMEM((4, *part), BF)] * 3
        + [pltpu.SemaphoreType.DMA((4, 2)), pltpu.SemaphoreType.DMA((4,))],
    )(order, mine, other)
    gm = after(gm, lines[0])
    sums = call(filter_kernel, shape((SMALL, TAPS), F32), [VMEM, VMEM], VMEM)(gm, pq)
    lines = [lines[0]] + [lax.ppermute(lines[i], "x", ring(4, i)) for i in (1, 2, 3)]
    sums = sums + lax.ppermute(sums, "core", ring(2, 1))
    sums = after(sums, lines[1])
    sums = [sums] + [lax.ppermute(sums, "x", ring(4, i)) for i in (1, 2, 3)]
    grad_query, grad_key, grad_value = call(
        finish_kernel, [shape((rows, width))] * 3, [VMEM] * 3, [VMEM] * 3
    )(k, v, grads)
    keep, send = call(
        line_kernel,
        [shape((panel + SMALL, outs_here))] * 2,
        [SMEM] * 2 + [VMEM] * 8,
        [VMEM] * 2,
        scratch=[pltpu.VMEM((4, SMALL, TAPS), F32)],
    )(source, zh.astype(jnp.int32).reshape(1), *lines, *sums)
    send = lax.ppermute(send, "zh", ring(2, 1))
    grad_weight, grad_filters, grad_gain = call(
        functools.partial(total_kernel, scale),
        [shape((outs_here, panel), F32), shape((groups, TAPS), F32), shape((panel // TAPS, TAPS), F32)],
        [VMEM] * 2,
        [VMEM] * 3,
    )(keep, send)
    return (
        grad_query[None],
        grad_key[None],
        grad_value[None],
        grad_weight,
        grad_filters,
        grad_gain.reshape(panel),
    )


def solution(mesh):
    fine = Mesh(mesh.devices.reshape(4, 2, 2, 2, 4), ("x", "zh", "core", "zl", "y"))
    stream = P(DP, SEQ, None)
    return jax.shard_map(
        shards,
        mesh=fine,
        in_specs=(stream, stream, stream, stream, P(DP, SEQ), P(), P()),
        out_specs=(stream, stream, stream, P(DP, SEQ), P(SEQ, None), P(SEQ)),
        check_vma=False,
    )
```

```python
import functools
import math

import jax
import jax.numpy as jnp
from jax import lax
from jax.experimental import pallas as pl
from jax.experimental.pallas import tpu as pltpu
from jax.sharding import Mesh
from jax.sharding import PartitionSpec as P

GROUP = 16
TAPS = 128
BLOCKS = 8
SMALL = 48
BF = jnp.bfloat16
F32 = jnp.float32
LIMIT = 60 * 1024 * 1024
DP = ("x", "zh", "core")
SEQ = ("zl", "y")

ANY = pl.BlockSpec(memory_space=pl.ANY)
SMEM = pl.BlockSpec(memory_space=pltpu.SMEM)
VMEM = pl.BlockSpec(memory_space=pltpu.VMEM)


def call(body, out_shape, in_specs, out_specs, scratch=(), micros=0):
    return pl.pallas_call(
        body,
        out_shape=out_shape,
        in_specs=in_specs,
        out_specs=out_specs,
        scratch_shapes=list(scratch),
        compiler_params=pltpu.CompilerParams(vmem_limit_bytes=LIMIT),
        cost_estimate=pl.CostEstimate(flops=1, bytes_accessed=1 + micros * 3000000, transcendentals=0),
    )


def shape(dims, dtype=BF):
    return jax.ShapeDtypeStruct(dims, dtype)


def table_kernel(panel_ref, filters_ref, gain_ref, table_ref, gain_out_ref):
    groups = table_ref.shape[0]
    panel = panel_ref[0]
    row = lax.broadcasted_iota(jnp.int32, (8, 2 * TAPS), 0)
    first = pl.multiple_of(panel * groups, groups)
    taps_all = filters_ref[pl.ds(first, groups), :].astype(F32)
    for g in range(groups):
        taps = jnp.broadcast_to(taps_all[g : g + 1, :], (8, TAPS))
        rows = jnp.concatenate([taps, jnp.zeros((8, TAPS), F32)], 1)
        for bit in (1, 2, 4):
            rows = jnp.where((row & bit) != 0, pltpu.roll(rows, bit, 1), rows)
        count = 8
        while count < TAPS:
            rows = jnp.concatenate([rows, pltpu.roll(rows, count, 1)], 0)
            count *= 2
        table_ref[g] = rows.astype(BF)
    gain_rows = gain_ref[panel]
    for i in range(gain_rows.shape[0]):
        gain_out_ref[TAPS * i : TAPS * (i + 1), :] = jnp.broadcast_to(
            gain_rows[i : i + 1, :], (TAPS, TAPS)
        ).T


def transpose_kernel(w_ref, out_ref):
    out_ref[...] = w_ref[...].astype(F32).T.astype(BF)


def prepare_kernel(q_ref, k_ref, v_ref, out_ref):
    width = out_ref.shape[2]
    for j in range(out_ref.shape[0]):
        cols = slice(j * width, (j + 1) * width)
        product = k_ref[:, cols].astype(F32) * v_ref[:, cols].astype(F32)
        out_ref[j, 0] = product.T.astype(BF)
        out_ref[j, 1] = q_ref[:, cols].astype(F32).T.astype(BF)


def forward_kernel(slot_ref, pq_ref, table_ref, gain_ref, mixed_ref, gated_ref):
    def one_group(g, carry):
        rows = pl.ds(pl.multiple_of(g * GROUP, GROUP), GROUP)
        x = [pq_ref[b, 0, rows, :] for b in range(BLOCKS)]
        zero = jnp.zeros((GROUP, TAPS), BF)
        lhs = jnp.concatenate(
            [jnp.concatenate(x, 0), jnp.concatenate([zero] + x[:-1], 0)], 1
        )
        table = table_ref[g]
        rhs = jnp.concatenate([table[:, :TAPS], table[:, TAPS:]], 0)
        conv = jnp.dot(lhs, rhs, preferred_element_type=F32)
        gain = gain_ref[rows, :]
        for b in range(BLOCKS):
            mixed = conv[GROUP * b : GROUP * (b + 1)] + gain * x[b].astype(F32)
            mixed_ref[b, rows, :] = mixed
            lanes = pl.ds(pl.multiple_of(slot_ref[b] * TAPS, TAPS), TAPS)
            gated_ref[rows, lanes] = (pq_ref[b, 1, rows, :].astype(F32) * mixed).astype(BF)
        return carry

    lax.fori_loop(0, table_ref.shape[0], one_group, 0, unroll=4)


def cot_copies(refs, held, sem_of, cols=slice(None)):
    copies = []
    half = TAPS // 2
    for zl in range(2):
        own, up, down, far_a, far_b = refs[5 * zl : 5 * zl + 5]
        for ref, k, first, count in (
            (own, 0, 0, TAPS),
            (up, 1, 0, TAPS),
            (far_a, 2, 0, half),
            (far_b, 2, half, half),
            (down, 3, 0, TAPS),
        ):
            slot = 4 * zl + k
            rows = slice(slot * TAPS + first, slot * TAPS + first + count)
            copies.append(
                pltpu.make_async_copy(ref.at[:, cols], held.at[rows, cols], sem_of(slot))
            )
    return copies


def product_kernel(core_ref, w_place_ref, place_ref, *refs):
    cot = refs[:10]
    gated_ref, w_refs, streams = refs[10], refs[11:19], refs[19:23]
    mine_ref, other_ref, gm_ref, out_ref = refs[23:27]
    held, w_held, total, grad_ref = refs[27:31]
    stream_held = refs[31:35]
    sems, w_sems, out_sems, stream_sems = refs[35:]
    mixed_ref, pq_ref, table_ref, gain_ref = stream_held
    blocks, channels, width = mine_ref.shape
    stripes = sems.shape[0]
    span = held.shape[1] // stripes
    each = blocks // stripes
    def stripe_start(n):
        for c in cot_copies(cot, held, lambda slot: sems.at[n], slice(span * n, span * (n + 1))):
            c.start()

    stripe_start(0)
    stripe_start(1)
    weights = []
    for d in range(2 * blocks):
        cols = pl.ds(pl.multiple_of(w_place_ref[d] * width, width), width)
        weights.append(
            pltpu.make_async_copy(w_refs[d // 2].at[d % 2], w_held.at[:, cols], w_sems.at[d])
        )
    ins = [
        pltpu.make_async_copy(ref, dst, stream_sems.at[i])
        for i, (ref, dst) in enumerate(zip(streams, stream_held))
    ]

    def out_copies(n):
        part = pl.ds(n * each, each)
        return [
            pltpu.make_async_copy(total.at[lax.rem(core_ref[0] + i, 2), part], ref.at[part], out_sems.at[i, n])
            for i, ref in enumerate((mine_ref, other_ref))
        ]

    for n in range(stripes):
        cols = slice(span * n, span * (n + 1))
        pltpu.make_async_copy(held.at[:, cols], held.at[:, cols], sems.at[n]).wait()
        if n + 2 < stripes:
            stripe_start(n + 2)
        for c in {stripes - 3: weights[:blocks], stripes - 2: weights[blocks:], stripes - 1: ins}.get(n, []):
            c.start()
        grad = jnp.dot(gated_ref[...], held[:, cols], preferred_element_type=F32)
        for i in range(2 * each):
            total[i % 2, n * each + i // 2] = grad[:, width * i : width * (i + 1)].astype(BF)
        for c in out_copies(n):
            c.start()
    for c in weights:
        c.wait()
    span = 4 * TAPS

    def tokens(n, carry):
        toks = pl.ds(pl.multiple_of(n * span, span), span)
        grad = lax.dot_general(
            w_held[...], held[toks, :], (((1,), (1,)), ((), ())), preferred_element_type=F32
        )
        for i in range(4):
            grad_ref[place_ref[4 * n + i]] = grad[:, TAPS * i : TAPS * (i + 1)]
        return carry

    lax.fori_loop(0, 2, tokens, 0)
    for c in ins:
        c.wait()

    def one_group(g, carry):
        rows = pl.ds(pl.multiple_of(g * GROUP, GROUP), GROUP)
        table = table_ref[g]
        gain = gain_ref[rows, :]
        zero = jnp.zeros((GROUP, TAPS), BF)
        x = []
        for b in range(BLOCKS):
            grad = grad_ref[b, rows, :]
            out_ref[b, 0, rows, :] = (grad * mixed_ref[b, rows, :]).astype(BF)
            x.append((grad * pq_ref[b, 1, rows, :].astype(F32)).astype(BF))
            gm_ref[b, rows, :] = x[b]
        lhs = jnp.concatenate(
            [jnp.concatenate(x, 0), jnp.concatenate(x[1:] + [zero], 0)], 1
        )
        conv = lax.dot_general(lhs, table, (((1,), (1,)), ((), ())), preferred_element_type=F32)
        for b in range(BLOCKS):
            result = conv[GROUP * b : GROUP * (b + 1)] + gain * x[b].astype(F32)
            out_ref[b, 1, rows, :] = result.astype(BF)
        return carry

    lax.fori_loop(0, table_ref.shape[0], one_group, 0, unroll=4)
    for n in range(stripes):
        for c in out_copies(n):
            c.wait()


def filter_kernel(gm_ref, pq_ref, out_ref):
    channels = gm_ref.shape[1]
    groups = channels // GROUP
    span = 2 * TAPS
    row = lax.broadcasted_iota(jnp.int32, (8, span), 0)

    def one_group(g, carry):
        rows = pl.ds(pl.multiple_of(g * GROUP, GROUP), GROUP)
        x = jnp.concatenate([pq_ref[b, 0, rows, :] for b in range(BLOCKS)], 0)
        y = [gm_ref[b, rows, :] for b in range(BLOCKS)]
        zero = jnp.zeros((GROUP, TAPS), BF)
        window = jnp.concatenate(
            [jnp.concatenate(y, 0), jnp.concatenate(y[1:] + [zero], 0)], 1
        )
        pairs = lax.dot_general(x, window, (((0,), (0,)), ((), ())), preferred_element_type=F32)
        count = TAPS
        while count > 8:
            count //= 2
            pairs = pairs[:count] + pltpu.roll(pairs[count:], span - count, 1)
        for bit in (4, 2, 1):
            pairs = jnp.where((row & bit) != 0, pltpu.roll(pairs, span - bit, 1), pairs)
        out_ref[pl.ds(g, 1), :] = jnp.sum(pairs, 0, keepdims=True)[:, :TAPS]
        return carry

    lax.fori_loop(0, groups, one_group, 0, unroll=8)
    for i in range(channels // TAPS):
        rows = slice(TAPS * i, TAPS * (i + 1))
        total = jnp.zeros((TAPS, TAPS), F32)
        for b in range(BLOCKS):
            total += gm_ref[b, rows, :].astype(F32) * pq_ref[b, 0, rows, :].astype(F32)
        out_ref[groups + i : groups + i + 1, :] = jnp.sum(total.T, 0, keepdims=True)
    first = groups + channels // TAPS
    out_ref[first:, :] = jnp.zeros((out_ref.shape[0] - first, TAPS), F32)


def put_small(ref, small):
    high = small.astype(BF)
    rows = slice(ref.shape[0] - small.shape[0], ref.shape[0])
    ref[rows, :TAPS] = high
    ref[rows, TAPS:] = (small - high.astype(F32)).astype(BF)


def get_small(piece):
    small = piece[piece.shape[0] - SMALL :].astype(F32)
    return small[:, :TAPS] + small[:, TAPS:]


def pair_kernel(order_ref, mine_ref, other_ref, *refs):
    outs = refs[:4]
    mine, other, lines, sems, out_sems = refs[4:]
    ins = []
    for i in range(4):
        part = pl.ds(order_ref[i] * 2, 2)
        ins.append([
            pltpu.make_async_copy(ref.at[part], held.at[i], sems.at[i, j])
            for j, (ref, held) in enumerate(((mine_ref, mine), (other_ref, other)))
        ])
        for c in ins[-1]:
            c.start()
    backs = []
    for i in range(4):
        for c in ins[i]:
            c.wait()
        lines[i] = mine[i] + other[i]
        backs.append(pltpu.make_async_copy(lines.at[i], outs[i], out_sems.at[i]))
        backs[-1].start()
    for c in backs:
        c.wait()


def line_kernel(source_ref, zh_ref, *refs):
    pieces, smalls, outs, held = refs[:4], refs[4:8], refs[8:10], refs[10]
    channels = pieces[0].shape[1]
    for i, piece in enumerate(smalls):
        held[source_ref[i]] = piece[...]
    small = ((held[0] + held[1]) + held[2]) + held[3]
    for out, zh in zip(outs, (zh_ref[0], 1 - zh_ref[0])):
        total = pieces[0][zh].astype(F32)
        for piece in pieces[1:]:
            total += piece[zh].astype(F32)
        out[:channels] = total.astype(BF)
        put_small(out, small)


def total_kernel(scale, mine_ref, other_ref, weight_ref, filter_ref, gain_ref):
    channels = weight_ref.shape[1]
    total = mine_ref[:channels].astype(F32) + other_ref[:channels].astype(F32)
    weight_ref[...] = (total * scale).T
    small = (get_small(mine_ref[...]) + get_small(other_ref[...])) * scale
    groups = filter_ref.shape[0]
    filter_ref[...] = small[:groups]
    gain_ref[...] = small[groups : groups + gain_ref.shape[0]]


def finish_kernel(k_ref, v_ref, grads_ref, gq_ref, gk_ref, gv_ref):
    width = grads_ref.shape[2]
    for j in range(grads_ref.shape[0]):
        cols = slice(j * width, (j + 1) * width)
        gq_ref[:, cols] = grads_ref[j, 0].astype(F32).T.astype(BF)
        gp = grads_ref[j, 1].astype(F32).T
        gk_ref[:, cols] = (gp * v_ref[:, cols].astype(F32)).astype(BF)
        gv_ref[:, cols] = (gp * k_ref[:, cols].astype(F32)).astype(BF)


SLOTS = [(d, k) for d in range(2) for k in range(4)]


def after(value, *others):
    return lax.optimization_barrier((value, *others))[0]


def ring(n, k):
    return [(i, (i + k) % n) for i in range(n)]


def numbers(values):
    return jnp.stack(values).astype(jnp.int32)


def shards(queries, key_input, value_input, cotangent, out_weight, filters, skip_gain):
    q, k, v, cot = queries[0], key_input[0], value_input[0], cotangent[0]
    rows, width = q.shape
    half = rows // 2
    panel = width // 8
    outs_here = out_weight.shape[0]
    length = rows * 8
    groups = panel // GROUP
    scale = 1.0 / math.sqrt(16 * length)
    x, zh, core, zl, y = (lax.axis_index(n) for n in ("x", "zh", "core", "zl", "y"))
    place = numbers([(zl ^ d) * 4 + (y - i) % 4 for d, i in SLOTS])
    slot_of = numbers([(zl ^ (p // 4)) * 4 + (y - p) % 4 for p in range(BLOCKS)])
    order = numbers([(x + i) % 4 for i in range(4)])
    source = numbers([(x - i) % 4 for i in range(4)])
    w_place = numbers(
        [((x - i) % 4 * 2 + (zh ^ d)) * 2 + (core ^ c) for c in range(2) for i in range(4) for d in range(2)]
    )
    stream = shape((8, 2, panel, rows))

    w_t = call(transpose_kernel, shape((panel, outs_here)), [VMEM], VMEM)(out_weight)
    pq = call(prepare_kernel, stream, [VMEM] * 3, VMEM)(q, k, v)
    w_other = after(lax.ppermute(w_t, "zh", ring(2, 1)), pq)
    w_t = jnp.stack([w_t, w_other])
    w_up, w_down = lax.ppermute(w_t, "x", ring(4, 1)), lax.ppermute(w_t, "x", ring(4, 3))
    w_far = lax.ppermute(after(w_t, w_up, w_down), "x", ring(4, 2))
    w_all = [w_t, w_up, w_far, w_down]
    w_all = w_all + [lax.ppermute(w, "core", ring(2, 1)) for w in w_all]

    own = cot
    own_z = lax.ppermute(after(own, pq), "zl", ring(2, 1))
    up = lax.ppermute(own, "y", ring(4, 1))
    down = lax.ppermute(own, "y", ring(4, -1))

    table, gain = call(
        table_kernel,
        [shape((groups, TAPS, 2 * TAPS)), shape((panel, TAPS), F32)],
        [SMEM, VMEM, VMEM],
        [VMEM, VMEM],
    )((zl * 4 + y).astype(jnp.int32).reshape(1), filters, skip_gain.reshape(8, panel // TAPS, TAPS))
    up, down, own_z, table = lax.optimization_barrier((up, down, own_z, table))
    far_a = lax.ppermute(up[:half], "y", ring(4, 1))
    far_b = lax.ppermute(down[half:], "y", ring(4, -1))
    up_z = lax.ppermute(own_z, "y", ring(4, 1))
    down_z = lax.ppermute(own_z, "y", ring(4, -1))
    far_a_z = lax.ppermute(far_a, "zl", ring(2, 1))
    far_b_z = lax.ppermute(far_b, "zl", ring(2, 1))
    cots = [own, up, down, far_a, far_b, own_z, up_z, down_z, far_a_z, far_b_z]
    pq = lax.all_to_all(pq, SEQ, split_axis=0, concat_axis=0, tiled=True)

    mixed, gated = call(
        forward_kernel,
        [shape((BLOCKS, panel, rows), F32), shape((panel, length))],
        [SMEM] + [VMEM] * 3,
        [VMEM] * 2,
    )(slot_of, pq, table, gain)

    by_core = (8, panel, outs_here)
    mine, other, gm, grads = call(
        product_kernel,
        [shape(by_core), shape(by_core), shape((BLOCKS, panel, rows)), stream],
        [SMEM] * 3 + [ANY] * 10 + [VMEM] + [ANY] * 12,
        [ANY, ANY, VMEM, VMEM],
        scratch=[
            pltpu.VMEM((length, width), BF),
            pltpu.VMEM((panel, width), BF),
            pltpu.VMEM((2, *by_core), BF),
            pltpu.VMEM((BLOCKS, panel, rows), F32),
            pltpu.VMEM((BLOCKS, panel, rows), F32),
            pltpu.VMEM(stream.shape, BF),
            pltpu.VMEM(table.shape, BF),
            pltpu.VMEM(gain.shape, F32),
            pltpu.SemaphoreType.DMA((4,)),
            pltpu.SemaphoreType.DMA((16,)),
            pltpu.SemaphoreType.DMA((2, 4)),
            pltpu.SemaphoreType.DMA((4,)),
        ],
        micros=100,
    )(core.astype(jnp.int32).reshape(1), w_place, place, *cots, gated, *w_all, mixed, pq, table, gain)
    other = lax.ppermute(other, "core", ring(2, 1))
    grads = lax.all_to_all(grads, SEQ, split_axis=0, concat_axis=0, tiled=True)

    part = (2, panel, outs_here)
    lines = call(
        pair_kernel,
        [shape(part)] * 4,
        [SMEM] + [ANY] * 2,
        [ANY] * 4,
        scratch=[pltpu.VMEM((4, *part), BF)] * 3
        + [pltpu.SemaphoreType.DMA((4, 2)), pltpu.SemaphoreType.DMA((4,))],
    )(order, mine, other)
    gm = after(gm, lines[0])
    sums = call(filter_kernel, shape((SMALL, TAPS), F32), [VMEM, VMEM], VMEM)(gm, pq)
    lines = [lines[0]] + [lax.ppermute(lines[i], "x", ring(4, i)) for i in (1, 2, 3)]
    sums = sums + lax.ppermute(sums, "core", ring(2, 1))
    sums = after(sums, lines[1])
    sums = [sums] + [lax.ppermute(sums, "x", ring(4, i)) for i in (1, 2, 3)]
    grad_query, grad_key, grad_value = call(
        finish_kernel, [shape((rows, width))] * 3, [VMEM] * 3, [VMEM] * 3
    )(k, v, grads)
    keep, send = call(
        line_kernel,
        [shape((panel + SMALL, outs_here))] * 2,
        [SMEM] * 2 + [VMEM] * 8,
        [VMEM] * 2,
        scratch=[pltpu.VMEM((4, SMALL, TAPS), F32)],
    )(source, zh.astype(jnp.int32).reshape(1), *lines, *sums)
    send = lax.ppermute(send, "zh", ring(2, 1))
    grad_weight, grad_filters, grad_gain = call(
        functools.partial(total_kernel, scale),
        [shape((outs_here, panel), F32), shape((groups, TAPS), F32), shape((panel // TAPS, TAPS), F32)],
        [VMEM] * 2,
        [VMEM] * 3,
    )(keep, send)
    return (
        grad_query[None],
        grad_key[None],
        grad_value[None],
        grad_weight,
        grad_filters,
        grad_gain.reshape(panel),
    )


def solution(mesh):
    fine = Mesh(mesh.devices.reshape(4, 2, 2, 2, 4), ("x", "zh", "core", "zl", "y"))
    stream = P(DP, SEQ, None)
    return jax.shard_map(
        shards,
        mesh=fine,
        in_specs=(stream, stream, stream, stream, P(DP, SEQ), P(), P()),
        out_specs=(stream, stream, stream, P(DP, SEQ), P(SEQ, None), P(SEQ)),
        check_vma=False,
    )
```

```python
import functools
import math

import jax
import jax.numpy as jnp
from jax import lax
from jax.experimental import pallas as pl
from jax.experimental.pallas import tpu as pltpu
from jax.sharding import Mesh
from jax.sharding import PartitionSpec as P

GROUP = 16
TAPS = 128
BLOCKS = 8
SMALL = 48
BF = jnp.bfloat16
F32 = jnp.float32
LIMIT = 60 * 1024 * 1024
DP = ("x", "zh", "core")
SEQ = ("zl", "y")

ANY = pl.BlockSpec(memory_space=pl.ANY)
SMEM = pl.BlockSpec(memory_space=pltpu.SMEM)
VMEM = pl.BlockSpec(memory_space=pltpu.VMEM)


def call(body, out_shape, in_specs, out_specs, scratch=(), micros=0):
    return pl.pallas_call(
        body,
        out_shape=out_shape,
        in_specs=in_specs,
        out_specs=out_specs,
        scratch_shapes=list(scratch),
        compiler_params=pltpu.CompilerParams(vmem_limit_bytes=LIMIT),
        cost_estimate=pl.CostEstimate(flops=1, bytes_accessed=1 + micros * 3000000, transcendentals=0),
    )


def shape(dims, dtype=BF):
    return jax.ShapeDtypeStruct(dims, dtype)


def table_kernel(panel_ref, filters_ref, gain_ref, table_ref, gain_out_ref):
    groups = table_ref.shape[0]
    panel = panel_ref[0]
    row = lax.broadcasted_iota(jnp.int32, (8, 2 * TAPS), 0)
    first = pl.multiple_of(panel * groups, groups)
    taps_all = filters_ref[pl.ds(first, groups), :].astype(F32)
    for g in range(groups):
        taps = jnp.broadcast_to(taps_all[g : g + 1, :], (8, TAPS))
        rows = jnp.concatenate([taps, jnp.zeros((8, TAPS), F32)], 1)
        for bit in (1, 2, 4):
            rows = jnp.where((row & bit) != 0, pltpu.roll(rows, bit, 1), rows)
        count = 8
        while count < TAPS:
            rows = jnp.concatenate([rows, pltpu.roll(rows, count, 1)], 0)
            count *= 2
        table_ref[g] = rows.astype(BF)
    gain_rows = gain_ref[panel]
    for i in range(gain_rows.shape[0]):
        gain_out_ref[TAPS * i : TAPS * (i + 1), :] = jnp.broadcast_to(
            gain_rows[i : i + 1, :], (TAPS, TAPS)
        ).T


def transpose_kernel(own_ref, other_ref, out_ref):
    for i, ref in enumerate((own_ref, other_ref)):
        out_ref[i] = ref[...].astype(F32).T.astype(BF)


def prepare_kernel(q_ref, k_ref, v_ref, out_ref):
    width = out_ref.shape[2]
    for j in range(out_ref.shape[0]):
        cols = slice(j * width, (j + 1) * width)
        product = k_ref[:, cols].astype(F32) * v_ref[:, cols].astype(F32)
        out_ref[j, 0] = product.T.astype(BF)
        out_ref[j, 1] = q_ref[:, cols].astype(F32).T.astype(BF)


def forward_kernel(slot_ref, pq_ref, table_ref, gain_ref, mixed_ref, gated_ref):
    def one_group(g, carry):
        rows = pl.ds(pl.multiple_of(g * GROUP, GROUP), GROUP)
        x = [pq_ref[b, 0, rows, :] for b in range(BLOCKS)]
        zero = jnp.zeros((GROUP, TAPS), BF)
        lhs = jnp.concatenate(
            [jnp.concatenate(x, 0), jnp.concatenate([zero] + x[:-1], 0)], 1
        )
        table = table_ref[g]
        rhs = jnp.concatenate([table[:, :TAPS], table[:, TAPS:]], 0)
        conv = jnp.dot(lhs, rhs, preferred_element_type=F32)
        gain = gain_ref[rows, :]
        for b in range(BLOCKS):
            mixed = conv[GROUP * b : GROUP * (b + 1)] + gain * x[b].astype(F32)
            mixed_ref[b, rows, :] = mixed
            lanes = pl.ds(pl.multiple_of(slot_ref[b] * TAPS, TAPS), TAPS)
            gated_ref[rows, lanes] = (pq_ref[b, 1, rows, :].astype(F32) * mixed).astype(BF)
        return carry

    lax.fori_loop(0, table_ref.shape[0], one_group, 0, unroll=4)


def cot_copies(refs, held, sem_of, cols=slice(None)):
    copies = []
    half = TAPS // 2
    for zl in range(2):
        own, up, down, far_a, far_b = refs[5 * zl : 5 * zl + 5]
        for ref, k, first, count in (
            (own, 0, 0, TAPS),
            (up, 1, 0, TAPS),
            (far_a, 2, 0, half),
            (far_b, 2, half, half),
            (down, 3, 0, TAPS),
        ):
            slot = 4 * zl + k
            rows = slice(slot * TAPS + first, slot * TAPS + first + count)
            copies.append(
                pltpu.make_async_copy(ref.at[:, cols], held.at[rows, cols], sem_of(slot))
            )
    return copies


def product_kernel(core_ref, w_place_ref, place_ref, *refs):
    cot = refs[:10]
    gated_in_ref, w_refs, streams = refs[10], refs[11:19], refs[19:23]
    mine_ref, other_ref, gm_out_ref, out_out_ref = refs[23:27]
    held, w_held, total, grad_ref = refs[27:31]
    stream_held = refs[31:35]
    gated_ref, gm_ref, out_ref = refs[35:38]
    sems, w_sems, out_sems, stream_sems, back_sems = refs[38:]
    mixed_ref, pq_ref, table_ref, gain_ref = stream_held
    blocks, channels, width = mine_ref.shape
    stripes = sems.shape[0]
    span = held.shape[1] // stripes
    each = blocks // stripes
    def stripe_start(n):
        for c in cot_copies(cot, held, lambda slot: sems.at[n], slice(span * n, span * (n + 1))):
            c.start()

    gated_in = pltpu.make_async_copy(gated_in_ref, gated_ref, back_sems.at[0, 0])
    gated_in.start()
    stripe_start(0)
    stripe_start(1)
    weights = []
    for d in range(2 * blocks):
        cols = pl.ds(pl.multiple_of(w_place_ref[d] * width, width), width)
        weights.append(
            pltpu.make_async_copy(w_refs[d // 2].at[d % 2], w_held.at[:, cols], w_sems.at[d])
        )
    ins = [
        pltpu.make_async_copy(ref, dst, stream_sems.at[i])
        for i, (ref, dst) in enumerate(zip(streams, stream_held))
    ]

    def out_copies(n):
        part = pl.ds(n * each, each)
        return [
            pltpu.make_async_copy(total.at[lax.rem(core_ref[0] + i, 2), part], ref.at[part], out_sems.at[i, n])
            for i, ref in enumerate((mine_ref, other_ref))
        ]

    gated_in.wait()
    for n in range(stripes):
        cols = slice(span * n, span * (n + 1))
        pltpu.make_async_copy(held.at[:, cols], held.at[:, cols], sems.at[n]).wait()
        if n + 2 < stripes:
            stripe_start(n + 2)
        for c in {stripes - 3: weights[:blocks], stripes - 2: weights[blocks:], stripes - 1: ins}.get(n, []):
            c.start()
        grad = jnp.dot(gated_ref[...], held[:, cols], preferred_element_type=F32)
        for i in range(2 * each):
            total[i % 2, n * each + i // 2] = grad[:, width * i : width * (i + 1)].astype(BF)
        for c in out_copies(n):
            c.start()
    for c in weights:
        c.wait()
    span = 4 * TAPS

    def tokens(n, carry):
        toks = pl.ds(pl.multiple_of(n * span, span), span)
        grad = lax.dot_general(
            w_held[...], held[toks, :], (((1,), (1,)), ((), ())), preferred_element_type=F32
        )
        for i in range(4):
            grad_ref[place_ref[4 * n + i]] = grad[:, TAPS * i : TAPS * (i + 1)]
        return carry

    lax.fori_loop(0, 2, tokens, 0)
    for c in ins:
        c.wait()

    def one_group(g, carry):
        rows = pl.ds(pl.multiple_of(g * GROUP, GROUP), GROUP)
        table = table_ref[g]
        gain = gain_ref[rows, :]
        zero = jnp.zeros((GROUP, TAPS), BF)
        x = []
        for b in range(BLOCKS):
            grad = grad_ref[b, rows, :]
            out_ref[b, 0, rows, :] = (grad * mixed_ref[b, rows, :]).astype(BF)
            x.append((grad * pq_ref[b, 1, rows, :].astype(F32)).astype(BF))
            gm_ref[b, rows, :] = x[b]
        lhs = jnp.concatenate(
            [jnp.concatenate(x, 0), jnp.concatenate(x[1:] + [zero], 0)], 1
        )
        conv = lax.dot_general(lhs, table, (((1,), (1,)), ((), ())), preferred_element_type=F32)
        for b in range(BLOCKS):
            result = conv[GROUP * b : GROUP * (b + 1)] + gain * x[b].astype(F32)
            out_ref[b, 1, rows, :] = result.astype(BF)
        return carry

    backs = []
    quarter = table_ref.shape[0] // 4
    for n in range(4):
        lax.fori_loop(quarter * n, quarter * (n + 1), one_group, 0, unroll=4)
        rows = slice(quarter * n * GROUP, quarter * (n + 1) * GROUP)
        backs.append(pltpu.make_async_copy(gm_ref.at[:, rows], gm_out_ref.at[:, rows], back_sems.at[1, n]))
        backs.append(
            pltpu.make_async_copy(out_ref.at[:, :, rows], out_out_ref.at[:, :, rows], back_sems.at[2, n])
        )
        for c in backs[-2:]:
            c.start()
    for c in backs:
        c.wait()
    for n in range(stripes):
        for c in out_copies(n):
            c.wait()


def filter_kernel(gm_ref, pq_ref, out_ref):
    channels = gm_ref.shape[1]
    groups = channels // GROUP
    span = 2 * TAPS
    row = lax.broadcasted_iota(jnp.int32, (8, span), 0)

    def one_group(g, carry):
        rows = pl.ds(pl.multiple_of(g * GROUP, GROUP), GROUP)
        x = jnp.concatenate([pq_ref[b, 0, rows, :] for b in range(BLOCKS)], 0)
        y = [gm_ref[b, rows, :] for b in range(BLOCKS)]
        zero = jnp.zeros((GROUP, TAPS), BF)
        window = jnp.concatenate(
            [jnp.concatenate(y, 0), jnp.concatenate(y[1:] + [zero], 0)], 1
        )
        pairs = lax.dot_general(x, window, (((0,), (0,)), ((), ())), preferred_element_type=F32)
        count = TAPS
        while count > 8:
            count //= 2
            pairs = pairs[:count] + pltpu.roll(pairs[count:], span - count, 1)
        for bit in (4, 2, 1):
            pairs = jnp.where((row & bit) != 0, pltpu.roll(pairs, span - bit, 1), pairs)
        out_ref[pl.ds(g, 1), :] = jnp.sum(pairs, 0, keepdims=True)[:, :TAPS]
        return carry

    lax.fori_loop(0, groups, one_group, 0, unroll=8)
    for i in range(channels // TAPS):
        rows = slice(TAPS * i, TAPS * (i + 1))
        total = jnp.zeros((TAPS, TAPS), F32)
        for b in range(BLOCKS):
            total += gm_ref[b, rows, :].astype(F32) * pq_ref[b, 0, rows, :].astype(F32)
        out_ref[groups + i : groups + i + 1, :] = jnp.sum(total.T, 0, keepdims=True)
    first = groups + channels // TAPS
    out_ref[first:, :] = jnp.zeros((out_ref.shape[0] - first, TAPS), F32)


def put_small(ref, small):
    high = small.astype(BF)
    rows = slice(ref.shape[0] - small.shape[0], ref.shape[0])
    ref[rows, :TAPS] = high
    ref[rows, TAPS:] = (small - high.astype(F32)).astype(BF)


def get_small(piece):
    small = piece[piece.shape[0] - SMALL :].astype(F32)
    return small[:, :TAPS] + small[:, TAPS:]


def pair_kernel(order_ref, mine_ref, other_ref, *refs):
    outs = refs[:4]
    mine, other, lines, sems, out_sems = refs[4:]
    ins = []
    for i in range(4):
        part = pl.ds(order_ref[i] * 2, 2)
        ins.append([
            pltpu.make_async_copy(ref.at[part], held.at[i], sems.at[i, j])
            for j, (ref, held) in enumerate(((mine_ref, mine), (other_ref, other)))
        ])
        for c in ins[-1]:
            c.start()
    backs = []
    for i in range(4):
        for c in ins[i]:
            c.wait()
        lines[i] = mine[i] + other[i]
        backs.append(pltpu.make_async_copy(lines.at[i], outs[i], out_sems.at[i]))
        backs[-1].start()
    for c in backs:
        c.wait()


def line_kernel(source_ref, zh_ref, *refs):
    pieces, smalls, outs, held = refs[:4], refs[4:8], refs[8:10], refs[10]
    channels = pieces[0].shape[1]
    for i, piece in enumerate(smalls):
        held[source_ref[i]] = piece[...]
    small = ((held[0] + held[1]) + held[2]) + held[3]
    for out, zh in zip(outs, (zh_ref[0], 1 - zh_ref[0])):
        total = pieces[0][zh].astype(F32)
        for piece in pieces[1:]:
            total += piece[zh].astype(F32)
        out[:channels] = total.astype(BF)
        put_small(out, small)


def total_kernel(scale, mine_ref, other_ref, weight_ref, filter_ref, gain_ref):
    channels = weight_ref.shape[1]
    total = mine_ref[:channels].astype(F32) + other_ref[:channels].astype(F32)
    weight_ref[...] = (total * scale).T
    small = (get_small(mine_ref[...]) + get_small(other_ref[...])) * scale
    groups = filter_ref.shape[0]
    filter_ref[...] = small[:groups]
    gain_ref[...] = small[groups : groups + gain_ref.shape[0]]


def finish_kernel(k_ref, v_ref, grads_ref, gq_ref, gk_ref, gv_ref):
    width = grads_ref.shape[2]
    for j in range(grads_ref.shape[0]):
        cols = slice(j * width, (j + 1) * width)
        gq_ref[:, cols] = grads_ref[j, 0].astype(F32).T.astype(BF)
        gp = grads_ref[j, 1].astype(F32).T
        gk_ref[:, cols] = (gp * v_ref[:, cols].astype(F32)).astype(BF)
        gv_ref[:, cols] = (gp * k_ref[:, cols].astype(F32)).astype(BF)


SLOTS = [(d, k) for d in range(2) for k in range(4)]


def after(value, *others):
    return lax.optimization_barrier((value, *others))[0]


def ring(n, k):
    return [(i, (i + k) % n) for i in range(n)]


def numbers(values):
    return jnp.stack(values).astype(jnp.int32)


def shards(queries, key_input, value_input, cotangent, out_weight, filters, skip_gain):
    q, k, v, cot = queries[0], key_input[0], value_input[0], cotangent[0]
    rows, width = q.shape
    half = rows // 2
    panel = width // 8
    outs_here = out_weight.shape[0]
    length = rows * 8
    groups = panel // GROUP
    scale = 1.0 / math.sqrt(16 * length)
    x, zh, core, zl, y = (lax.axis_index(n) for n in ("x", "zh", "core", "zl", "y"))
    place = numbers([(zl ^ d) * 4 + (y - i) % 4 for d, i in SLOTS])
    slot_of = numbers([(zl ^ (p // 4)) * 4 + (y - p) % 4 for p in range(BLOCKS)])
    order = numbers([(x + i) % 4 for i in range(4)])
    source = numbers([(x - i) % 4 for i in range(4)])
    w_place = numbers(
        [((x - i) % 4 * 2 + (zh ^ d)) * 2 + (core ^ c) for c in range(2) for i in range(4) for d in range(2)]
    )
    stream = shape((8, 2, panel, rows))

    pq = call(prepare_kernel, stream, [VMEM] * 3, VMEM)(q, k, v)
    w_other = after(lax.ppermute(out_weight, "zh", ring(2, 1)), pq)
    w_t = call(transpose_kernel, shape((2, panel, outs_here)), [VMEM] * 2, VMEM)(out_weight, w_other)
    w_up, w_down = lax.ppermute(w_t, "x", ring(4, 1)), lax.ppermute(w_t, "x", ring(4, 3))
    w_far = lax.ppermute(after(w_t, w_up, w_down), "x", ring(4, 2))
    w_all = [w_t, w_up, w_far, w_down]
    w_all = w_all + [lax.ppermute(w, "core", ring(2, 1)) for w in w_all]

    own = cot
    own_z = lax.ppermute(after(own, pq), "zl", ring(2, 1))
    up = lax.ppermute(own, "y", ring(4, 1))
    down = lax.ppermute(own, "y", ring(4, -1))

    table, gain = call(
        table_kernel,
        [shape((groups, TAPS, 2 * TAPS)), shape((panel, TAPS), F32)],
        [SMEM, VMEM, VMEM],
        [VMEM, VMEM],
    )((zl * 4 + y).astype(jnp.int32).reshape(1), filters, skip_gain.reshape(8, panel // TAPS, TAPS))
    up, down, own_z, table = lax.optimization_barrier((up, down, own_z, table))
    far_a = lax.ppermute(up[:half], "y", ring(4, 1))
    far_b = lax.ppermute(down[half:], "y", ring(4, -1))
    up_z = lax.ppermute(own_z, "y", ring(4, 1))
    down_z = lax.ppermute(own_z, "y", ring(4, -1))
    far_a_z = lax.ppermute(far_a, "zl", ring(2, 1))
    far_b_z = lax.ppermute(far_b, "zl", ring(2, 1))
    cots = [own, up, down, far_a, far_b, own_z, up_z, down_z, far_a_z, far_b_z]
    pq = lax.all_to_all(pq, SEQ, split_axis=0, concat_axis=0, tiled=True)

    mixed, gated = call(
        forward_kernel,
        [shape((BLOCKS, panel, rows), F32), shape((panel, length))],
        [SMEM] + [VMEM] * 3,
        [VMEM] * 2,
    )(slot_of, pq, table, gain)

    by_core = (8, panel, outs_here)
    mine, other, gm, grads = call(
        product_kernel,
        [shape(by_core), shape(by_core), shape((BLOCKS, panel, rows)), stream],
        [SMEM] * 3 + [ANY] * 23,
        [ANY] * 4,
        scratch=[
            pltpu.VMEM((length, width), BF),
            pltpu.VMEM((panel, width), BF),
            pltpu.VMEM((2, *by_core), BF),
            pltpu.VMEM((BLOCKS, panel, rows), F32),
            pltpu.VMEM((BLOCKS, panel, rows), F32),
            pltpu.VMEM(stream.shape, BF),
            pltpu.VMEM(table.shape, BF),
            pltpu.VMEM(gain.shape, F32),
            pltpu.VMEM((panel, length), BF),
            pltpu.VMEM((BLOCKS, panel, rows), BF),
            pltpu.VMEM(stream.shape, BF),
            pltpu.SemaphoreType.DMA((4,)),
            pltpu.SemaphoreType.DMA((16,)),
            pltpu.SemaphoreType.DMA((2, 4)),
            pltpu.SemaphoreType.DMA((4,)),
            pltpu.SemaphoreType.DMA((3, 4)),
        ],
        micros=100,
    )(core.astype(jnp.int32).reshape(1), w_place, place, *cots, gated, *w_all, mixed, pq, table, gain)
    other = lax.ppermute(other, "core", ring(2, 1))
    grads = lax.all_to_all(grads, SEQ, split_axis=0, concat_axis=0, tiled=True)

    part = (2, panel, outs_here)
    lines = call(
        pair_kernel,
        [shape(part)] * 4,
        [SMEM] + [ANY] * 2,
        [ANY] * 4,
        scratch=[pltpu.VMEM((4, *part), BF)] * 3
        + [pltpu.SemaphoreType.DMA((4, 2)), pltpu.SemaphoreType.DMA((4,))],
    )(order, mine, other)
    gm = after(gm, lines[0])
    sums = call(filter_kernel, shape((SMALL, TAPS), F32), [VMEM, VMEM], VMEM)(gm, pq)
    lines = [lines[0]] + [lax.ppermute(lines[i], "x", ring(4, i)) for i in (1, 2, 3)]
    sums = sums + lax.ppermute(sums, "core", ring(2, 1))
    sums = after(sums, lines[1])
    sums = [sums] + [lax.ppermute(sums, "x", ring(4, i)) for i in (1, 2, 3)]
    grad_query, grad_key, grad_value = call(
        finish_kernel, [shape((rows, width))] * 3, [VMEM] * 3, [VMEM] * 3
    )(k, v, grads)
    keep, send = call(
        line_kernel,
        [shape((panel + SMALL, outs_here))] * 2,
        [SMEM] * 2 + [VMEM] * 8,
        [VMEM] * 2,
        scratch=[pltpu.VMEM((4, SMALL, TAPS), F32)],
    )(source, zh.astype(jnp.int32).reshape(1), *lines, *sums)
    send = lax.ppermute(send, "zh", ring(2, 1))
    grad_weight, grad_filters, grad_gain = call(
        functools.partial(total_kernel, scale),
        [shape((outs_here, panel), F32), shape((groups, TAPS), F32), shape((panel // TAPS, TAPS), F32)],
        [VMEM] * 2,
        [VMEM] * 3,
    )(keep, send)
    return (
        grad_query[None],
        grad_key[None],
        grad_value[None],
        grad_weight,
        grad_filters,
        grad_gain.reshape(panel),
    )


def solution(mesh):
    fine = Mesh(mesh.devices.reshape(4, 2, 2, 2, 4), ("x", "zh", "core", "zl", "y"))
    stream = P(DP, SEQ, None)
    return jax.shard_map(
        shards,
        mesh=fine,
        in_specs=(stream, stream, stream, stream, P(DP, SEQ), P(), P()),
        out_specs=(stream, stream, stream, P(DP, SEQ), P(SEQ, None), P(SEQ)),
        check_vma=False,
    )
```

```python
import functools
import math

import jax
import jax.numpy as jnp
from jax import lax
from jax.experimental import pallas as pl
from jax.experimental.pallas import tpu as pltpu
from jax.sharding import Mesh
from jax.sharding import PartitionSpec as P

GROUP = 16
TAPS = 128
BLOCKS = 8
SMALL = 48
BF = jnp.bfloat16
F32 = jnp.float32
LIMIT = 60 * 1024 * 1024
DP = ("x", "zh", "core")
SEQ = ("zl", "y")

ANY = pl.BlockSpec(memory_space=pl.ANY)
SMEM = pl.BlockSpec(memory_space=pltpu.SMEM)
VMEM = pl.BlockSpec(memory_space=pltpu.VMEM)


def call(body, out_shape, in_specs, out_specs, scratch=(), micros=0):
    return pl.pallas_call(
        body,
        out_shape=out_shape,
        in_specs=in_specs,
        out_specs=out_specs,
        scratch_shapes=list(scratch),
        compiler_params=pltpu.CompilerParams(vmem_limit_bytes=LIMIT),
        cost_estimate=pl.CostEstimate(flops=1, bytes_accessed=1 + micros * 3000000, transcendentals=0),
    )


def shape(dims, dtype=BF):
    return jax.ShapeDtypeStruct(dims, dtype)


def table_kernel(panel_ref, filters_ref, gain_ref, table_ref, gain_out_ref):
    groups = table_ref.shape[0]
    panel = panel_ref[0]
    row = lax.broadcasted_iota(jnp.int32, (8, 2 * TAPS), 0)
    first = pl.multiple_of(panel * groups, groups)
    taps_all = filters_ref[pl.ds(first, groups), :].astype(F32)
    for g in range(groups):
        taps = jnp.broadcast_to(taps_all[g : g + 1, :], (8, TAPS))
        rows = jnp.concatenate([taps, jnp.zeros((8, TAPS), F32)], 1)
        for bit in (1, 2, 4):
            rows = jnp.where((row & bit) != 0, pltpu.roll(rows, bit, 1), rows)
        count = 8
        while count < TAPS:
            rows = jnp.concatenate([rows, pltpu.roll(rows, count, 1)], 0)
            count *= 2
        table_ref[g] = rows.astype(BF)
    gain_rows = gain_ref[panel]
    for i in range(gain_rows.shape[0]):
        gain_out_ref[TAPS * i : TAPS * (i + 1), :] = jnp.broadcast_to(
            gain_rows[i : i + 1, :], (TAPS, TAPS)
        ).T


def transpose_kernel(own_ref, other_ref, out_ref):
    for i, ref in enumerate((own_ref, other_ref)):
        out_ref[i] = ref[...].astype(F32).T.astype(BF)


def prepare_kernel(q_ref, k_ref, v_ref, out_ref, held, result, sems, out_sems):
    blocks, _, width, _ = out_ref.shape
    ins = []
    for j in range(blocks):
        cols = slice(j * width, (j + 1) * width)
        ins.append([
            pltpu.make_async_copy(ref.at[:, cols], held.at[i, :, cols], sems.at[j, i])
            for i, ref in enumerate((q_ref, k_ref, v_ref))
        ])
        for c in ins[-1]:
            c.start()
    backs = []
    for j in range(blocks):
        cols = slice(j * width, (j + 1) * width)
        for c in ins[j]:
            c.wait()
        product = held[1, :, cols].astype(F32) * held[2, :, cols].astype(F32)
        result[j, 0] = product.T.astype(BF)
        result[j, 1] = held[0, :, cols].astype(F32).T.astype(BF)
        backs.append(pltpu.make_async_copy(result.at[j], out_ref.at[j], out_sems.at[j]))
        backs[-1].start()
    for c in backs:
        c.wait()


def forward_kernel(slot_ref, pq_ref, table_ref, gain_ref, mixed_ref, gated_ref):
    def one_group(g, carry):
        rows = pl.ds(pl.multiple_of(g * GROUP, GROUP), GROUP)
        x = [pq_ref[b, 0, rows, :] for b in range(BLOCKS)]
        zero = jnp.zeros((GROUP, TAPS), BF)
        lhs = jnp.concatenate(
            [jnp.concatenate(x, 0), jnp.concatenate([zero] + x[:-1], 0)], 1
        )
        table = table_ref[g]
        rhs = jnp.concatenate([table[:, :TAPS], table[:, TAPS:]], 0)
        conv = jnp.dot(lhs, rhs, preferred_element_type=F32)
        gain = gain_ref[rows, :]
        for b in range(BLOCKS):
            mixed = conv[GROUP * b : GROUP * (b + 1)] + gain * x[b].astype(F32)
            mixed_ref[b, rows, :] = mixed
            lanes = pl.ds(pl.multiple_of(slot_ref[b] * TAPS, TAPS), TAPS)
            gated_ref[rows, lanes] = (pq_ref[b, 1, rows, :].astype(F32) * mixed).astype(BF)
        return carry

    lax.fori_loop(0, table_ref.shape[0], one_group, 0, unroll=4)


def cot_copies(refs, held, sem_of, cols=slice(None)):
    copies = []
    half = TAPS // 2
    for zl in range(2):
        own, up, down, far_a, far_b = refs[5 * zl : 5 * zl + 5]
        for ref, k, first, count in (
            (own, 0, 0, TAPS),
            (up, 1, 0, TAPS),
            (far_a, 2, 0, half),
            (far_b, 2, half, half),
            (down, 3, 0, TAPS),
        ):
            slot = 4 * zl + k
            rows = slice(slot * TAPS + first, slot * TAPS + first + count)
            copies.append(
                pltpu.make_async_copy(ref.at[:, cols], held.at[rows, cols], sem_of(slot))
            )
    return copies


def product_kernel(core_ref, w_place_ref, place_ref, *refs):
    cot = refs[:10]
    gated_in_ref, w_refs, streams = refs[10], refs[11:19], refs[19:23]
    mine_ref, other_ref, gm_out_ref, out_out_ref = refs[23:27]
    held, w_held, total, grad_ref = refs[27:31]
    stream_held = refs[31:35]
    gated_ref, gm_ref, out_ref = refs[35:38]
    sems, w_sems, out_sems, stream_sems, back_sems = refs[38:]
    mixed_ref, pq_ref, table_ref, gain_ref = stream_held
    blocks, channels, width = mine_ref.shape
    stripes = sems.shape[0]
    span = held.shape[1] // stripes
    each = blocks // stripes
    def stripe_start(n):
        for c in cot_copies(cot, held, lambda slot: sems.at[n], slice(span * n, span * (n + 1))):
            c.start()

    gated_in = pltpu.make_async_copy(gated_in_ref, gated_ref, back_sems.at[0, 0])
    gated_in.start()
    stripe_start(0)
    stripe_start(1)
    weights = []
    for d in range(2 * blocks):
        cols = pl.ds(pl.multiple_of(w_place_ref[d] * width, width), width)
        weights.append(
            pltpu.make_async_copy(w_refs[d // 2].at[d % 2], w_held.at[:, cols], w_sems.at[d])
        )
    ins = [
        pltpu.make_async_copy(ref, dst, stream_sems.at[i])
        for i, (ref, dst) in enumerate(zip(streams, stream_held))
    ]

    def out_copies(n):
        part = pl.ds(n * each, each)
        return [
            pltpu.make_async_copy(total.at[lax.rem(core_ref[0] + i, 2), part], ref.at[part], out_sems.at[i, n])
            for i, ref in enumerate((mine_ref, other_ref))
        ]

    gated_in.wait()
    for n in range(stripes):
        cols = slice(span * n, span * (n + 1))
        pltpu.make_async_copy(held.at[:, cols], held.at[:, cols], sems.at[n]).wait()
        if n + 2 < stripes:
            stripe_start(n + 2)
        for c in {stripes - 3: weights[:blocks], stripes - 2: weights[blocks:], stripes - 1: ins}.get(n, []):
            c.start()
        grad = jnp.dot(gated_ref[...], held[:, cols], preferred_element_type=F32)
        for i in range(2 * each):
            total[i % 2, n * each + i // 2] = grad[:, width * i : width * (i + 1)].astype(BF)
        for c in out_copies(n):
            c.start()
    for c in weights:
        c.wait()
    span = 4 * TAPS

    def tokens(n, carry):
        toks = pl.ds(pl.multiple_of(n * span, span), span)
        grad = lax.dot_general(
            w_held[...], held[toks, :], (((1,), (1,)), ((), ())), preferred_element_type=F32
        )
        for i in range(4):
            grad_ref[place_ref[4 * n + i]] = grad[:, TAPS * i : TAPS * (i + 1)]
        return carry

    lax.fori_loop(0, 2, tokens, 0)
    for c in ins:
        c.wait()

    def one_group(g, carry):
        rows = pl.ds(pl.multiple_of(g * GROUP, GROUP), GROUP)
        table = table_ref[g]
        gain = gain_ref[rows, :]
        zero = jnp.zeros((GROUP, TAPS), BF)
        x = []
        for b in range(BLOCKS):
            grad = grad_ref[b, rows, :]
            out_ref[b, 0, rows, :] = (grad * mixed_ref[b, rows, :]).astype(BF)
            x.append((grad * pq_ref[b, 1, rows, :].astype(F32)).astype(BF))
            gm_ref[b, rows, :] = x[b]
        lhs = jnp.concatenate(
            [jnp.concatenate(x, 0), jnp.concatenate(x[1:] + [zero], 0)], 1
        )
        conv = lax.dot_general(lhs, table, (((1,), (1,)), ((), ())), preferred_element_type=F32)
        for b in range(BLOCKS):
            result = conv[GROUP * b : GROUP * (b + 1)] + gain * x[b].astype(F32)
            out_ref[b, 1, rows, :] = result.astype(BF)
        return carry

    backs = []
    quarter = table_ref.shape[0] // 4
    for n in range(4):
        lax.fori_loop(quarter * n, quarter * (n + 1), one_group, 0, unroll=4)
        rows = slice(quarter * n * GROUP, quarter * (n + 1) * GROUP)
        backs.append(pltpu.make_async_copy(gm_ref.at[:, rows], gm_out_ref.at[:, rows], back_sems.at[1, n]))
        backs.append(
            pltpu.make_async_copy(out_ref.at[:, :, rows], out_out_ref.at[:, :, rows], back_sems.at[2, n])
        )
        for c in backs[-2:]:
            c.start()
    for c in backs:
        c.wait()
    for n in range(stripes):
        for c in out_copies(n):
            c.wait()


def filter_kernel(gm_ref, pq_ref, out_ref):
    channels = gm_ref.shape[1]
    groups = channels // GROUP
    span = 2 * TAPS
    row = lax.broadcasted_iota(jnp.int32, (8, span), 0)

    def one_group(g, carry):
        rows = pl.ds(pl.multiple_of(g * GROUP, GROUP), GROUP)
        x = jnp.concatenate([pq_ref[b, 0, rows, :] for b in range(BLOCKS)], 0)
        y = [gm_ref[b, rows, :] for b in range(BLOCKS)]
        zero = jnp.zeros((GROUP, TAPS), BF)
        window = jnp.concatenate(
            [jnp.concatenate(y, 0), jnp.concatenate(y[1:] + [zero], 0)], 1
        )
        pairs = lax.dot_general(x, window, (((0,), (0,)), ((), ())), preferred_element_type=F32)
        count = TAPS
        while count > 8:
            count //= 2
            pairs = pairs[:count] + pltpu.roll(pairs[count:], span - count, 1)
        for bit in (4, 2, 1):
            pairs = jnp.where((row & bit) != 0, pltpu.roll(pairs, span - bit, 1), pairs)
        out_ref[pl.ds(g, 1), :] = jnp.sum(pairs, 0, keepdims=True)[:, :TAPS]
        return carry

    lax.fori_loop(0, groups, one_group, 0, unroll=8)
    for i in range(channels // TAPS):
        rows = slice(TAPS * i, TAPS * (i + 1))
        total = jnp.zeros((TAPS, TAPS), F32)
        for b in range(BLOCKS):
            total += gm_ref[b, rows, :].astype(F32) * pq_ref[b, 0, rows, :].astype(F32)
        out_ref[groups + i : groups + i + 1, :] = jnp.sum(total.T, 0, keepdims=True)
    first = groups + channels // TAPS
    out_ref[first:, :] = jnp.zeros((out_ref.shape[0] - first, TAPS), F32)


def put_small(ref, small):
    high = small.astype(BF)
    rows = slice(ref.shape[0] - small.shape[0], ref.shape[0])
    ref[rows, :TAPS] = high
    ref[rows, TAPS:] = (small - high.astype(F32)).astype(BF)


def get_small(piece):
    small = piece[piece.shape[0] - SMALL :].astype(F32)
    return small[:, :TAPS] + small[:, TAPS:]


def pair_kernel(order_ref, mine_ref, other_ref, *refs):
    outs = refs[:4]
    mine, other, lines, sems, out_sems = refs[4:]
    ins = []
    for i in range(4):
        part = pl.ds(order_ref[i] * 2, 2)
        ins.append([
            pltpu.make_async_copy(ref.at[part], held.at[i], sems.at[i, j])
            for j, (ref, held) in enumerate(((mine_ref, mine), (other_ref, other)))
        ])
        for c in ins[-1]:
            c.start()
    backs = []
    for i in range(4):
        for c in ins[i]:
            c.wait()
        lines[i] = mine[i] + other[i]
        backs.append(pltpu.make_async_copy(lines.at[i], outs[i], out_sems.at[i]))
        backs[-1].start()
    for c in backs:
        c.wait()


def line_kernel(source_ref, zh_ref, *refs):
    pieces, smalls, outs, held = refs[:4], refs[4:8], refs[8:10], refs[10]
    channels = pieces[0].shape[1]
    for i, piece in enumerate(smalls):
        held[source_ref[i]] = piece[...]
    small = ((held[0] + held[1]) + held[2]) + held[3]
    for out, zh in zip(outs, (zh_ref[0], 1 - zh_ref[0])):
        total = pieces[0][zh].astype(F32)
        for piece in pieces[1:]:
            total += piece[zh].astype(F32)
        out[:channels] = total.astype(BF)
        put_small(out, small)


def total_kernel(scale, mine_ref, other_ref, weight_ref, filter_ref, gain_ref):
    channels = weight_ref.shape[1]
    total = mine_ref[:channels].astype(F32) + other_ref[:channels].astype(F32)
    weight_ref[...] = (total * scale).T
    small = (get_small(mine_ref[...]) + get_small(other_ref[...])) * scale
    groups = filter_ref.shape[0]
    filter_ref[...] = small[:groups]
    gain_ref[...] = small[groups : groups + gain_ref.shape[0]]


def finish_kernel(k_ref, v_ref, grads_ref, gq_ref, gk_ref, gv_ref):
    width = grads_ref.shape[2]
    for j in range(grads_ref.shape[0]):
        cols = slice(j * width, (j + 1) * width)
        gq_ref[:, cols] = grads_ref[j, 0].astype(F32).T.astype(BF)
        gp = grads_ref[j, 1].astype(F32).T
        gk_ref[:, cols] = (gp * v_ref[:, cols].astype(F32)).astype(BF)
        gv_ref[:, cols] = (gp * k_ref[:, cols].astype(F32)).astype(BF)


SLOTS = [(d, k) for d in range(2) for k in range(4)]


def after(value, *others):
    return lax.optimization_barrier((value, *others))[0]


def ring(n, k):
    return [(i, (i + k) % n) for i in range(n)]


def numbers(values):
    return jnp.stack(values).astype(jnp.int32)


def shards(queries, key_input, value_input, cotangent, out_weight, filters, skip_gain):
    q, k, v, cot = queries[0], key_input[0], value_input[0], cotangent[0]
    rows, width = q.shape
    half = rows // 2
    panel = width // 8
    outs_here = out_weight.shape[0]
    length = rows * 8
    groups = panel // GROUP
    scale = 1.0 / math.sqrt(16 * length)
    x, zh, core, zl, y = (lax.axis_index(n) for n in ("x", "zh", "core", "zl", "y"))
    place = numbers([(zl ^ d) * 4 + (y - i) % 4 for d, i in SLOTS])
    slot_of = numbers([(zl ^ (p // 4)) * 4 + (y - p) % 4 for p in range(BLOCKS)])
    order = numbers([(x + i) % 4 for i in range(4)])
    source = numbers([(x - i) % 4 for i in range(4)])
    w_place = numbers(
        [((x - i) % 4 * 2 + (zh ^ d)) * 2 + (core ^ c) for c in range(2) for i in range(4) for d in range(2)]
    )
    stream = shape((8, 2, panel, rows))

    pq = call(
        prepare_kernel,
        stream,
        [ANY] * 3,
        ANY,
        scratch=[
            pltpu.VMEM((3, rows, width), BF),
            pltpu.VMEM(stream.shape, BF),
            pltpu.SemaphoreType.DMA((8, 3)),
            pltpu.SemaphoreType.DMA((8,)),
        ],
    )(q, k, v)
    w_other = after(lax.ppermute(out_weight, "zh", ring(2, 1)), pq)
    w_t = call(transpose_kernel, shape((2, panel, outs_here)), [VMEM] * 2, VMEM)(out_weight, w_other)
    w_up, w_down = lax.ppermute(w_t, "x", ring(4, 1)), lax.ppermute(w_t, "x", ring(4, 3))
    w_far = lax.ppermute(after(w_t, w_up, w_down), "x", ring(4, 2))
    w_all = [w_t, w_up, w_far, w_down]
    w_all = w_all + [lax.ppermute(w, "core", ring(2, 1)) for w in w_all]

    own = cot
    own_z = lax.ppermute(after(own, pq), "zl", ring(2, 1))
    up = lax.ppermute(own, "y", ring(4, 1))
    down = lax.ppermute(own, "y", ring(4, -1))

    table, gain = call(
        table_kernel,
        [shape((groups, TAPS, 2 * TAPS)), shape((panel, TAPS), F32)],
        [SMEM, VMEM, VMEM],
        [VMEM, VMEM],
    )((zl * 4 + y).astype(jnp.int32).reshape(1), filters, skip_gain.reshape(8, panel // TAPS, TAPS))
    up, down, own_z, table = lax.optimization_barrier((up, down, own_z, table))
    far_a = lax.ppermute(up[:half], "y", ring(4, 1))
    far_b = lax.ppermute(down[half:], "y", ring(4, -1))
    up_z = lax.ppermute(own_z, "y", ring(4, 1))
    down_z = lax.ppermute(own_z, "y", ring(4, -1))
    far_a_z = lax.ppermute(far_a, "zl", ring(2, 1))
    far_b_z = lax.ppermute(far_b, "zl", ring(2, 1))
    cots = [own, up, down, far_a, far_b, own_z, up_z, down_z, far_a_z, far_b_z]
    pq = lax.all_to_all(pq, SEQ, split_axis=0, concat_axis=0, tiled=True)

    mixed, gated = call(
        forward_kernel,
        [shape((BLOCKS, panel, rows), F32), shape((panel, length))],
        [SMEM] + [VMEM] * 3,
        [VMEM] * 2,
    )(slot_of, pq, table, gain)

    by_core = (8, panel, outs_here)
    mine, other, gm, grads = call(
        product_kernel,
        [shape(by_core), shape(by_core), shape((BLOCKS, panel, rows)), stream],
        [SMEM] * 3 + [ANY] * 23,
        [ANY] * 4,
        scratch=[
            pltpu.VMEM((length, width), BF),
            pltpu.VMEM((panel, width), BF),
            pltpu.VMEM((2, *by_core), BF),
            pltpu.VMEM((BLOCKS, panel, rows), F32),
            pltpu.VMEM((BLOCKS, panel, rows), F32),
            pltpu.VMEM(stream.shape, BF),
            pltpu.VMEM(table.shape, BF),
            pltpu.VMEM(gain.shape, F32),
            pltpu.VMEM((panel, length), BF),
            pltpu.VMEM((BLOCKS, panel, rows), BF),
            pltpu.VMEM(stream.shape, BF),
            pltpu.SemaphoreType.DMA((4,)),
            pltpu.SemaphoreType.DMA((16,)),
            pltpu.SemaphoreType.DMA((2, 4)),
            pltpu.SemaphoreType.DMA((4,)),
            pltpu.SemaphoreType.DMA((3, 4)),
        ],
        micros=100,
    )(core.astype(jnp.int32).reshape(1), w_place, place, *cots, gated, *w_all, mixed, pq, table, gain)
    other = lax.ppermute(other, "core", ring(2, 1))
    grads = lax.all_to_all(grads, SEQ, split_axis=0, concat_axis=0, tiled=True)

    part = (2, panel, outs_here)
    lines = call(
        pair_kernel,
        [shape(part)] * 4,
        [SMEM] + [ANY] * 2,
        [ANY] * 4,
        scratch=[pltpu.VMEM((4, *part), BF)] * 3
        + [pltpu.SemaphoreType.DMA((4, 2)), pltpu.SemaphoreType.DMA((4,))],
    )(order, mine, other)
    gm = after(gm, lines[0])
    sums = call(filter_kernel, shape((SMALL, TAPS), F32), [VMEM, VMEM], VMEM)(gm, pq)
    lines = [lines[0]] + [lax.ppermute(lines[i], "x", ring(4, i)) for i in (1, 2, 3)]
    sums = sums + lax.ppermute(sums, "core", ring(2, 1))
    sums = after(sums, lines[1])
    sums = [sums] + [lax.ppermute(sums, "x", ring(4, i)) for i in (1, 2, 3)]
    grad_query, grad_key, grad_value = call(
        finish_kernel, [shape((rows, width))] * 3, [VMEM] * 3, [VMEM] * 3
    )(k, v, grads)
    keep, send = call(
        line_kernel,
        [shape((panel + SMALL, outs_here))] * 2,
        [SMEM] * 2 + [VMEM] * 8,
        [VMEM] * 2,
        scratch=[pltpu.VMEM((4, SMALL, TAPS), F32)],
    )(source, zh.astype(jnp.int32).reshape(1), *lines, *sums)
    send = lax.ppermute(send, "zh", ring(2, 1))
    grad_weight, grad_filters, grad_gain = call(
        functools.partial(total_kernel, scale),
        [shape((outs_here, panel), F32), shape((groups, TAPS), F32), shape((panel // TAPS, TAPS), F32)],
        [VMEM] * 2,
        [VMEM] * 3,
    )(keep, send)
    return (
        grad_query[None],
        grad_key[None],
        grad_value[None],
        grad_weight,
        grad_filters,
        grad_gain.reshape(panel),
    )


def solution(mesh):
    fine = Mesh(mesh.devices.reshape(4, 2, 2, 2, 4), ("x", "zh", "core", "zl", "y"))
    stream = P(DP, SEQ, None)
    return jax.shard_map(
        shards,
        mesh=fine,
        in_specs=(stream, stream, stream, stream, P(DP, SEQ), P(), P()),
        out_specs=(stream, stream, stream, P(DP, SEQ), P(SEQ, None), P(SEQ)),
        check_vma=False,
    )
```
